512 devices in a mesh: dp: 32 (over y_lo, z), fsdp: 16 (over y_hi, x, core).
Axes of the slice: x: 4, y: 4 (y_hi: 2, y_lo: 2; y = y_hi * 2 + y_lo), z: 16, core: 2. Of those that a mesh axis runs over, the one named last changes fastest.
Arguments:
- policy_out: bfloat16 [640, 2560], P('fsdp'), may hold values from -0.25 to 0.25
- frozen_out: bfloat16 [640, 2560], P('fsdp'), may hold values from -0.25 to 0.25
- qkv_current: bfloat16 [131072, 896], P(('dp', 'fsdp')), may hold values from -8.125 to 8.125
- segment_current: int32 [131072], P(('dp', 'fsdp')), may hold values from 0 to 15, as said below
- grad_output: bfloat16 [131072, 2560], P(('dp', 'fsdp')), may hold values from -6 to 6
- query_key_value_next: bfloat16 [131072, 896], P(('dp', 'fsdp')), may hold values from -8.125 to 8.125
- document_next: int32 [131072], P(('dp', 'fsdp')), may hold values from 0 to 15, as said below
- block_counts: int32 [32, 16], P('dp', 'fsdp'), may hold values from 0 to 2, as said below
- move_plan: int32 [32, 16, 5], P('dp', 'fsdp'), may hold values from 0 to 1, as said below
Outputs:
- qkv_gradient: bfloat16 [131072, 896], P(('dp', 'fsdp'))
- weight_grad: bfloat16 [640, 2560], P('fsdp')
- frozen_layer_output: bfloat16 [131072, 2560], P(('dp', 'fsdp'))
The draws below stay inside these ranges and needn't reach their ends.
Inputs may be any that keep to these rules, and one draw needn't show every extreme that they name: `segment_current`: within each aligned block of 128 rows the ids start at 0, never fall, and change only at multiples of 8 rows. `document_next`: within each aligned block of 128 rows the ids start at 0, never fall, and change only at multiples of 8 rows. `block_counts`: A device's live blocks are its first slots. `move_plan`: of two partners at a step at most one sends; no device ever holds more than 2 or fewer than 0 live blocks.
All inputs are finite; a program needn't handle non-finite values.
Results may differ from the reference program's by a relative error of at most 0.019.
Values may be sent and summed in bfloat16 or wider, within the bound.
No kernel may reach another device: no remote copies, remote signals or barrier semaphores. Data moves between devices by JAX's collectives and lax.ppermute only.
A program may use at most 64 MiB of HBM per device.

```python
import functools
import math
import jax
import jax.numpy as jnp
from jax import lax

D = 2560
HD = 128
HQ = 5
ALIGNED_ROWS = 128
POL_BLK = 2
SLOT_NUMBER = 2
QW = 640
QUERY_KEY_VALUE = 896
STEPS = 5
ROWS_POL = 131072
ROWS_REF = 131072
N_DP = 32
N_FSDP = 16


def draw_qkv_current(key, part):
    key = jax.random.fold_in(key, 11)
    key_first = jax.random.fold_in(key, 0)
    row_summation = N_DP * N_FSDP * POL_BLK * ALIGNED_ROWS
    base_rows = jnp.clip(jax.random.normal(key_first, (row_summation, (HQ + 2) * HD), jnp.float32), -4.0, 4.0)
    return base_rows.astype(jnp.bfloat16)


def draw_query_key_value_next(key, part):
    key = jax.random.fold_in(key, 12)
    key_first = jax.random.fold_in(key, 0)
    row_summation = N_DP * N_FSDP * SLOT_NUMBER * ALIGNED_ROWS
    base_rows = jnp.clip(jax.random.normal(key_first, (row_summation, (HQ + 2) * HD), jnp.float32), -4.0, 4.0)
    return base_rows.astype(jnp.bfloat16)


def segment_distribution(key, row_summation):
    group_count = ALIGNED_ROWS // 8
    bound_flags = (jax.random.randint(key, (row_summation // ALIGNED_ROWS, group_count), 0, 3) == 0).astype(jnp.int32)
    bound_flags = bound_flags.at[:, 0].set(1).at[0, :].set(1)
    segment_ids = jnp.cumsum(bound_flags, axis=1) - 1
    return jnp.repeat(segment_ids, 8, axis=1).reshape(row_summation).astype(jnp.int32)


def draw_segment_current(key, part):
    key = jax.random.fold_in(key, 21)
    return segment_distribution(key, N_DP * N_FSDP * POL_BLK * ALIGNED_ROWS)


def draw_document_next(key, part):
    key = jax.random.fold_in(key, 22)
    return segment_distribution(key, N_DP * N_FSDP * SLOT_NUMBER * ALIGNED_ROWS)


def shared_plan(key):
    key = jax.random.fold_in(key, 31)
    key_first, key_second = jax.random.split(key)
    light_burden = jax.random.randint(key_first, (N_DP, N_FSDP), 0, 2)
    heavy_marker = jax.random.randint(key_second, (N_DP, N_FSDP), 0, 4) == 0
    count_table = jnp.where(heavy_marker, SLOT_NUMBER, light_burden).astype(jnp.int32)
    count_table = count_table.at[0].set(0).at[1].set(SLOT_NUMBER)
    current = count_table
    device_ids = jnp.arange(N_DP)
    sends = []
    for level in range(STEPS):
        partner = jnp.bitwise_xor(device_ids, 1 << level)
        opposite = current[partner]
        send_count = jnp.where(current > opposite, (current - opposite) // 2, 0)
        sends.append(send_count)
        current = current - send_count + send_count[partner]
    return (count_table, jnp.stack(sends, axis=2).astype(jnp.int32))


def draw_block_counts(key, part):
    count_table, plan_table = shared_plan(key)
    return count_table


def draw_move_plan(key, part):
    count_table, plan_table = shared_plan(key)
    return plan_table


def level_of(key, dims, shards, low, largest):
    factor_of = 1.0
    for axis_at, shards_of in shards:
        steps = jax.random.uniform(jax.random.fold_in(jax.random.fold_in(key, 6), axis_at), (shards_of,), jnp.float32, low / len(shards), largest / len(shards))
        factor_of = factor_of * jnp.repeat(jnp.exp(steps), dims[axis_at] // shards_of).reshape((-1,) + (1,) * (len(dims) - 1 - axis_at))
    return factor_of


def gaussian(own_key, extent, scale, bound, cuts=(), dtype=jnp.bfloat16):
    drawn = jax.random.normal(own_key, extent, jnp.float32) * scale
    if len(cuts) > 0:
        drawn = level_of(own_key, extent, cuts, -0.22, 0.18) * drawn
    return jnp.clip(drawn, min=-bound, max=bound).astype(dtype)


def setup_inputs(seed: int = 0) -> dict:
    arg_keys = jax.random.split(jax.random.key(seed), 10)
    return {
        "policy_out": gaussian(arg_keys[0], (QW, D), QW ** -0.5, 0.25, ((0, 16),)),
        "frozen_out": gaussian(arg_keys[1], (QW, D), QW ** -0.5, 0.25, ((0, 16),)),
        "qkv_current": draw_qkv_current(jax.random.fold_in(arg_keys[9], 71), 0),
        "segment_current": draw_segment_current(jax.random.fold_in(arg_keys[9], 71), 0),
        "grad_output": gaussian(arg_keys[4], (ROWS_POL, D), 1.0, 6.0, ((0, 512),)),
        "query_key_value_next": draw_query_key_value_next(jax.random.fold_in(arg_keys[9], 71), 0),
        "document_next": draw_document_next(jax.random.fold_in(arg_keys[9], 71), 0),
        "block_counts": draw_block_counts(jax.random.fold_in(arg_keys[9], 71), 0),
        "move_plan": draw_move_plan(jax.random.fold_in(arg_keys[9], 71), 0),
    }


masked_score = -1e+30

def split_heads(qkv_rows):
    blocks = qkv_rows.shape[0] // ALIGNED_ROWS
    query_width = HQ * HD
    query_matrix = qkv_rows[:, :query_width].reshape(blocks, ALIGNED_ROWS, HQ, HD).astype(jnp.float32)
    key_matrix = qkv_rows[:, query_width:query_width + HD].reshape(blocks, ALIGNED_ROWS, HD).astype(jnp.float32)
    value_matrix = qkv_rows[:, query_width + HD:].reshape(blocks, ALIGNED_ROWS, HD).astype(jnp.float32)
    return (query_matrix, key_matrix, value_matrix)

def attend_over_blocks(qkv_rows, segment_ids):
    query_matrix, key_matrix, value_matrix = split_heads(qkv_rows)
    blocks = query_matrix.shape[0]
    scale_multiplier = 1.0 / math.sqrt(HD)
    score_matrix = jnp.einsum('ofam,ozm->oafz', query_matrix, key_matrix) * scale_multiplier
    positions = jnp.arange(ALIGNED_ROWS)
    segment_block = segment_ids.reshape(blocks, ALIGNED_ROWS)
    allowed = (positions[:, None] >= positions[None, :])[None] & (segment_block[:, :, None] == segment_block[:, None, :])
    score_matrix = jnp.where(allowed[:, None], score_matrix, masked_score)
    row_max = lax.optimization_barrier(jnp.max(score_matrix, axis=-1, keepdims=True))
    exp_scores = jnp.exp(score_matrix - row_max)
    softmax_full = exp_scores / lax.optimization_barrier(jnp.sum(exp_scores, axis=-1, keepdims=True))
    softmax_reduced = lax.optimization_barrier(softmax_full.astype(jnp.bfloat16))
    output_rows = jnp.einsum('gpsa,gan->gspn', softmax_reduced.astype(jnp.float32), value_matrix)
    attention_map = output_rows.reshape(blocks * ALIGNED_ROWS, HQ * HD).astype(jnp.bfloat16)
    return (attention_map, softmax_full, softmax_reduced)

def attend_backward(qkv_rows, softmax_full, softmax_reduced, grad_attention):
    query_matrix, key_matrix, value_matrix = split_heads(qkv_rows)
    blocks = query_matrix.shape[0]
    scale_multiplier = 1.0 / math.sqrt(HD)
    output_gradient = grad_attention.reshape(blocks, ALIGNED_ROWS, HQ, HD).astype(jnp.float32)
    probability_gradient = jnp.einsum('ofam,ozm->oafz', output_gradient, value_matrix)
    centre = lax.optimization_barrier(jnp.sum(softmax_full * probability_gradient, axis=-1, keepdims=True))
    score_gradient = softmax_full * (probability_gradient - centre)
    query_gradient = jnp.einsum('gpsa,gan->gspn', score_gradient, key_matrix, precision=lax.Precision.HIGHEST) * scale_multiplier
    key_gradient = jnp.einsum('xzrl,xrzw->xlw', score_gradient, query_matrix, precision=lax.Precision.HIGHEST) * scale_multiplier
    value_gradient = jnp.einsum('xzrl,xrzw->xlw', softmax_reduced.astype(jnp.float32), output_gradient)
    row_count = blocks * ALIGNED_ROWS
    joined = jnp.concatenate([query_gradient.reshape(row_count, HQ * HD), key_gradient.reshape(row_count, HD), value_gradient.reshape(row_count, HD)], axis=1)
    return joined.astype(jnp.bfloat16)

def take_outgoing(slot_contents, top_start, send_count, slot_capacity):
    pieces = []
    for offset in range(slot_capacity):
        slot_index = jnp.clip(top_start + offset, 0, slot_contents.shape[0] - 1).astype(jnp.int32)
        chosen_block = lax.dynamic_index_in_dim(slot_contents, slot_index, 0, keepdims=False)
        pieces.append(jnp.where(offset < send_count, chosen_block, jnp.zeros_like(chosen_block)))
    return jnp.stack(pieces)

def place_incoming(slot_contents, incoming, top_start, recv_count):
    slot_ids = jnp.arange(slot_contents.shape[0])
    for offset in range(incoming.shape[0]):
        hit_mask = (slot_ids == top_start + offset) & (offset < recv_count)
        hit_mask = hit_mask.reshape((-1,) + (1,) * (slot_contents.ndim - 1))
        slot_contents = jnp.where(hit_mask, incoming[offset][None], slot_contents)
    return slot_contents

def reference(policy_out, frozen_out, qkv_current, segment_current, grad_output, query_key_value_next, document_next, block_counts, move_plan):
    group_rows = N_FSDP * POL_BLK * ALIGNED_ROWS
    qkv_groups = qkv_current.reshape(N_DP, group_rows, QUERY_KEY_VALUE)
    segment_groups = segment_current.reshape(N_DP, group_rows)
    grad_groups = grad_output.reshape(N_DP, group_rows, D)

    def policy_group(inputs):
        qkv_rows, segment_ids, grad_rows = inputs
        attention_map, softmax_full, softmax_reduced = attend_over_blocks(qkv_rows, segment_ids)
        grad_attention = jnp.dot(grad_rows, policy_out.T, preferred_element_type=jnp.float32).astype(jnp.bfloat16)
        qkv_grad = attend_backward(qkv_rows, softmax_full, softmax_reduced, grad_attention)
        terms = jnp.einsum('frc,frd->fcd', attention_map.reshape(N_FSDP, POL_BLK * ALIGNED_ROWS, QW).astype(jnp.float32), grad_rows.reshape(N_FSDP, POL_BLK * ALIGNED_ROWS, D).astype(jnp.float32))
        rounded = lax.optimization_barrier(terms.astype(jnp.bfloat16)).astype(jnp.float32)
        return (qkv_grad, lax.optimization_barrier(jnp.sum(rounded, axis=0)))
    qkv_grads, group_sums = lax.map(policy_group, (qkv_groups, segment_groups, grad_groups))
    weight_grad = (lax.optimization_barrier(jnp.sum(group_sums, axis=0)) * (1.0 / (N_DP * N_FSDP))).astype(jnp.bfloat16)
    slot_capacity = SLOT_NUMBER // 2
    slot_contents = query_key_value_next.reshape(N_DP, N_FSDP, SLOT_NUMBER, ALIGNED_ROWS, QUERY_KEY_VALUE)
    slot_documents = document_next.reshape(N_DP, N_FSDP, SLOT_NUMBER, ALIGNED_ROWS)
    count_table = block_counts.astype(jnp.int32)
    device_ids = jnp.arange(N_DP)
    take_all = jax.vmap(jax.vmap(functools.partial(take_outgoing, slot_capacity=slot_capacity)))
    place_all = jax.vmap(jax.vmap(place_incoming))
    for level in range(STEPS):
        partner = jnp.bitwise_xor(device_ids, 1 << level)
        send_count = move_plan[:, :, level].astype(jnp.int32)
        top_start = count_table - send_count
        out_data = take_all(slot_contents, top_start, send_count)
        out_segments = take_all(slot_documents, top_start, send_count)
        recv_count = send_count[partner]
        slot_contents = place_all(slot_contents, out_data[partner], top_start, recv_count)
        slot_documents = place_all(slot_documents, out_segments[partner], top_start, recv_count)
        count_table = top_start + recv_count

    def frozen_group(inputs):
        slot_row_block, document_rows, live_tally_count = inputs
        attention_map = attend_over_blocks(slot_row_block.reshape(N_FSDP * SLOT_NUMBER * ALIGNED_ROWS, QUERY_KEY_VALUE), document_rows.reshape(N_FSDP * SLOT_NUMBER * ALIGNED_ROWS))[0]
        product = jnp.dot(attention_map, frozen_out, preferred_element_type=jnp.float32).astype(jnp.bfloat16)
        live_marker = jnp.arange(SLOT_NUMBER)[None, :] < live_tally_count[:, None]
        active_rows = jnp.repeat(live_marker.reshape(N_FSDP * SLOT_NUMBER), ALIGNED_ROWS)
        return jnp.where(active_rows[:, None], product, jnp.zeros_like(product))
    frozen_rows = lax.map(frozen_group, (slot_contents, slot_documents, count_table))
    return (qkv_grads.reshape(ROWS_POL, QUERY_KEY_VALUE), weight_grad, frozen_rows.reshape(ROWS_REF, D))
```

```python
import math

import jax
import jax.numpy as jnp
from jax import lax
from jax.experimental import pallas as pl
from jax.experimental.pallas import tpu as pltpu
from jax.sharding import PartitionSpec as P

HD = 128
HQ = 5
ALIGNED_ROWS = 128
SLOT_NUMBER = 2
QW = HQ * HD
QKV = (HQ + 2) * HD
D = 2560
SCALE = 1.0 / math.sqrt(HD)
MASKED = -1e30
VMEM = 48 * 1024 * 1024

NN = (((1,), (0,)), ((), ()))
NT = (((1,), (1,)), ((), ()))
TN = (((0,), (0,)), ((), ()))


def dot(a, b, dims):
    return lax.dot_general(a, b, dims, preferred_element_type=jnp.float32)


def block_probs(x_ref, rows, allowed, h):
    q = x_ref[rows, h * HD : (h + 1) * HD]
    k = x_ref[rows, QW : QW + HD]
    s = jnp.where(allowed, dot(q, k, NT) * SCALE, MASKED)
    e = jnp.exp(s - jnp.max(s, axis=-1, keepdims=True))
    return e / jnp.sum(e, axis=-1, keepdims=True)


def allowed_pairs(seg_ref, b):
    key_seg = jnp.broadcast_to(seg_ref[b : b + 1, :].astype(jnp.float32), (ALIGNED_ROWS, ALIGNED_ROWS))
    query_pos = lax.broadcasted_iota(jnp.int32, key_seg.shape, 0)
    key_pos = lax.broadcasted_iota(jnp.int32, key_seg.shape, 1)
    return (query_pos >= key_pos) & (key_seg == key_seg.T)


def forward_kernel(cur_ref, cur_seg_ref, nxt_ref, nxt_seg_ref, order_ref, cur_out, nxt_out, prob_out, attn_ref):
    for b in range(2):
        rows = slice(b * ALIGNED_ROWS, (b + 1) * ALIGNED_ROWS)
        allowed = allowed_pairs(cur_seg_ref, b)
        for h in range(HQ):
            p = block_probs(cur_ref, rows, allowed, h)
            prob_out[h, rows, :] = p
            v = cur_ref[rows, QW + HD :]
            attn_ref[rows, h * HD : (h + 1) * HD] = dot(p.astype(jnp.bfloat16), v, NN).astype(jnp.bfloat16)
    cur_out[...] = dot(attn_ref[...], order_ref[...], NN).astype(jnp.bfloat16)
    for b in range(2):
        rows = slice(b * ALIGNED_ROWS, (b + 1) * ALIGNED_ROWS)
        allowed = allowed_pairs(nxt_seg_ref, b)
        for h in range(HQ):
            p = block_probs(nxt_ref, rows, allowed, h)
            v = nxt_ref[rows, QW + HD :]
            nxt_out[rows, h * HD : (h + 1) * HD] = dot(p.astype(jnp.bfloat16), v, NN).astype(jnp.bfloat16)


def forward_attention(qkv_current, segment_current, qkv_next, document_next, order):
    rows = qkv_current.shape[0]
    return pl.pallas_call(
        forward_kernel,
        out_shape=(
            jax.ShapeDtypeStruct((rows, QW), jnp.bfloat16),
            jax.ShapeDtypeStruct((rows, QW), jnp.bfloat16),
            jax.ShapeDtypeStruct((HQ, rows, HD), jnp.float32),
        ),
        scratch_shapes=[pltpu.VMEM((rows, QW), jnp.bfloat16)],
        compiler_params=pltpu.CompilerParams(vmem_limit_bytes=VMEM),
        cost_estimate=pl.CostEstimate(flops=10**9, bytes_accessed=3 * 10**6, transcendentals=10**6),
        name="forward_attention",
    )(qkv_current, segment_current, qkv_next, document_next, order)


def backward_kernel(x_ref, prob_ref, g_ref, w_ref, out_ref, dk_ref, dv_ref):
    h = pl.program_id(0)

    @pl.when(h == 0)
    def _():
        dk_ref[...] = jnp.zeros_like(dk_ref)
        dv_ref[...] = jnp.zeros_like(dv_ref)

    columns = pl.ds(pl.multiple_of(h * HD, HD), HD)
    grad_attention = dot(g_ref[...], w_ref[...], NT).astype(jnp.bfloat16)
    for b in range(2):
        rows = slice(b * ALIGNED_ROWS, (b + 1) * ALIGNED_ROWS)
        ga = grad_attention[rows]
        q = x_ref[rows, columns]
        k = x_ref[rows, QW : QW + HD]
        v = x_ref[rows, QW + HD :]
        p = prob_ref[rows, :]
        dp = dot(ga, v, NT)
        ds = p * (dp - jnp.sum(p * dp, axis=-1, keepdims=True))
        high = ds.astype(jnp.bfloat16)
        low = (ds - high.astype(jnp.float32)).astype(jnp.bfloat16)
        out_ref[rows, columns] = ((dot(high, k, NN) + dot(low, k, NN)) * SCALE).astype(jnp.bfloat16)
        dk_ref[rows, :] += dot(high, q, TN) + dot(low, q, TN)
        dv_ref[rows, :] += dot(p.astype(jnp.bfloat16), ga, TN)

    @pl.when(h == HQ - 1)
    def _():
        out_ref[:, QW : QW + HD] = (dk_ref[...] * SCALE).astype(jnp.bfloat16)
        out_ref[:, QW + HD :] = dv_ref[...].astype(jnp.bfloat16)


def backward_attention(qkv_current, probs, grad_output, weights):
    rows = qkv_current.shape[0]
    return pl.pallas_call(
        backward_kernel,
        grid=(HQ,),
        in_specs=[
            pl.BlockSpec((rows, QKV), lambda h: (0, 0)),
            pl.BlockSpec((None, rows, HD), lambda h: (h, 0, 0)),
            pl.BlockSpec((rows, D), lambda h: (0, 0)),
            pl.BlockSpec((HD, D), lambda h: (h, 0)),
        ],
        out_specs=pl.BlockSpec((rows, QKV), lambda h: (0, 0)),
        out_shape=jax.ShapeDtypeStruct((rows, QKV), jnp.bfloat16),
        scratch_shapes=[pltpu.VMEM((rows, HD), jnp.float32), pltpu.VMEM((rows, HD), jnp.float32)],
        compiler_params=pltpu.CompilerParams(vmem_limit_bytes=VMEM),
        cost_estimate=pl.CostEstimate(flops=2 * 10**9, bytes_accessed=6 * 10**6, transcendentals=0),
        name="backward_attention",
    )(qkv_current, probs, grad_output, weights)


def frozen_kernel(live_ref, a_ref, w_ref, out_ref):
    rows = lax.broadcasted_iota(jnp.int32, out_ref.shape, 0)
    product = dot(a_ref[...], w_ref[...], NN)
    out_ref[...] = jnp.where(rows < live_ref[0] * ALIGNED_ROWS, product, 0.0).astype(jnp.bfloat16)


def frozen_projection(live, attention, weights):
    rows = attention.shape[0]
    width = 512
    return pl.pallas_call(
        frozen_kernel,
        grid=(D // width,),
        in_specs=[
            pl.BlockSpec(memory_space=pltpu.SMEM),
            pl.BlockSpec((rows, QW), lambda i: (0, 0)),
            pl.BlockSpec((QW, width), lambda i: (0, D // width + i)),
        ],
        out_specs=pl.BlockSpec((rows, width), lambda i: (0, i)),
        out_shape=jax.ShapeDtypeStruct((rows, D), jnp.bfloat16),
        compiler_params=pltpu.CompilerParams(vmem_limit_bytes=VMEM),
        cost_estimate=pl.CostEstimate(flops=10**9, bytes_accessed=5 * 10**6, transcendentals=0),
        name="frozen_projection",
    )(live, attention, weights)


N_DP = 32
N_FSDP = 16


def fsdp_pairs(flip, x_step):
    def target(j):
        j ^= flip
        return (j & 9) | (((j >> 1 & 3) + x_step) % 4 << 1)

    return [(j, target(j)) for j in range(N_FSDP)]


def all_pairs(dp_flip, fsdp_flip):
    return [
        (d * N_FSDP + j, (d ^ dp_flip) * N_FSDP + (j ^ fsdp_flip)) for d in range(N_DP) for j in range(N_FSDP)
    ]


def swap(a, dp_flip, fsdp_flip=0):
    return lax.ppermute(a, ("dp", "fsdp"), all_pairs(dp_flip, fsdp_flip))


def add(*terms):
    return sum(t.astype(jnp.float32) for t in terms).astype(jnp.bfloat16)


def leaving_order(me):
    rows = QW // N_FSDP
    natural = jnp.arange(QW, dtype=jnp.int32)
    j, k = natural // rows, natural % rows
    flip = j ^ me
    place = (flip & 1) * 8 + (((j >> 1) - (me >> 1)) & 3) * 2 + (flip >> 3)
    return (natural[None, :] == (place * rows + k)[:, None]).astype(jnp.bfloat16)


def reduce_weight_grad(attention, grad_output, y_lo, z_lo):
    half = QW // 2
    terms = dot(attention[:, half:], grad_output, TN).astype(jnp.bfloat16)
    other = lax.ppermute(terms, "fsdp", fsdp_pairs(1, 0))
    total = add(dot(attention[:, :half], grad_output, TN).astype(jnp.bfloat16), other)
    chunks = total.reshape(4, half // 4, D)
    total = add(chunks[0], *(lax.ppermute(chunks[s], "fsdp", fsdp_pairs(0, s)) for s in (1, 2, 3)))
    own, far = total[: half // 8], total[half // 8 :]

    def halves(a, flag):
        left, right = jnp.split(a, 2, axis=1)
        return jnp.where(flag, right, left), jnp.where(flag, left, right)

    own_keep, own_give = halves(own, y_lo == 1)
    far_keep, far_give = halves(far, y_lo == 1)
    total = add(own_keep, swap(own_give, 16), swap(far_keep, 0, 8), swap(far_give, 16, 8))
    keep, give = halves(total, z_lo == 1)
    total = add(keep, swap(give, 1))
    total = add(total, swap(total, 2))
    total = add(total, swap(total, 4))
    total = total.astype(jnp.float32) + swap(total, 8).astype(jnp.float32)
    total = (total * (1.0 / (N_DP * N_FSDP))).astype(jnp.bfloat16)

    def joined(a, b, flag):
        return jnp.where(flag, jnp.concatenate([b, a], axis=1), jnp.concatenate([a, b], axis=1))

    near = joined(total, swap(total, 1), z_lo == 1)
    away = joined(swap(total, 16), swap(total, 17), z_lo == 1)
    return joined(near, away, y_lo == 1)


def move_blocks(attention, live, plan):
    slots = attention.reshape(SLOT_NUMBER, ALIGNED_ROWS, QW)
    for level in range(N_DP.bit_length() - 1):
        count = plan[level]
        top = live - count
        block = jnp.where(top >= 1, slots[1], slots[0])
        flag = jnp.full((16, QW), count, jnp.bfloat16)
        arrived = swap(jnp.concatenate([block, flag], axis=0), 1 << level)
        received = arrived[ALIGNED_ROWS, 0].astype(jnp.int32)
        block = arrived[:ALIGNED_ROWS]
        slots = jnp.stack(
            [jnp.where((received > 0) & (top == s), block, slots[s]) for s in range(SLOT_NUMBER)]
        )
        live = top + received
    return slots.reshape(SLOT_NUMBER * ALIGNED_ROWS, QW), live


def body(
    policy_out,
    frozen_out,
    qkv_current,
    segment_current,
    grad_output,
    query_key_value_next,
    document_next,
    block_counts,
    move_plan,
):
    me = lax.axis_index("fsdp")
    group = lax.axis_index("dp")
    weights = lax.all_gather(
        jnp.concatenate([policy_out, frozen_out], axis=1), "fsdp", axis=0, tiled=True
    )
    attention, next_attention, probs = forward_attention(
        qkv_current,
        segment_current.reshape(2, ALIGNED_ROWS),
        query_key_value_next,
        document_next.reshape(SLOT_NUMBER, ALIGNED_ROWS),
        leaving_order(me),
    )
    weight_grad = reduce_weight_grad(attention, grad_output, group >> 4, group & 1)
    moved, live = move_blocks(next_attention, block_counts[0, 0], move_plan[0, 0])
    qkv_gradient = backward_attention(qkv_current, probs, grad_output, weights)
    frozen_layer_output = frozen_projection(live.reshape(1), moved, weights)
    return (qkv_gradient, weight_grad, frozen_layer_output)


def solution(mesh):
    return jax.shard_map(
        body,
        mesh=mesh,
        in_specs=(
            P("fsdp", None),
            P("fsdp", None),
            P(("dp", "fsdp"), None),
            P(("dp", "fsdp")),
            P(("dp", "fsdp"), None),
            P(("dp", "fsdp"), None),
            P(("dp", "fsdp")),
            P("dp", "fsdp"),
            P("dp", "fsdp", None),
        ),
        out_specs=(P(("dp", "fsdp"), None), P("fsdp", None), P(("dp", "fsdp"), None)),
        check_vma=False,
    )
```

```python
import functools
import math

import jax
import jax.numpy as jnp
from jax import lax
from jax.experimental import pallas as pl
from jax.experimental.pallas import tpu as pltpu
from jax.sharding import PartitionSpec as P

HD = 128
HQ = 5
ALIGNED_ROWS = 128
SLOT_NUMBER = 2
QW = HQ * HD
QKV = (HQ + 2) * HD
D = 2560
SCALE = 1.0 / math.sqrt(HD)
MASKED = -1e30
ABSENT = 1024.0
COSTS = {f"move_step_{level}": (flops * 10**9, 0) for level, flops in ((1, 4), (2, 4), (3, 16), (4, 8))}
N_DP = 32
N_FSDP = 16
VMEM = 20 * 1024 * 1024

NN = (((1,), (0,)), ((), ()))
NT = (((1,), (1,)), ((), ()))
TN = (((0,), (0,)), ((), ()))


def dot(a, b, dims):
    return lax.dot_general(a, b, dims, preferred_element_type=jnp.float32)


def block_probs(x_ref, rows, allowed, h):
    q = x_ref[rows, h * HD : (h + 1) * HD]
    k = x_ref[rows, QW : QW + HD]
    s = jnp.where(allowed, dot(q, k, NT) * SCALE, MASKED)
    e = jnp.exp(s - jnp.max(s, axis=-1, keepdims=True))
    return e / jnp.sum(e, axis=-1, keepdims=True)


def allowed_pairs(seg_ref, b):
    key_seg = jnp.broadcast_to(seg_ref[b : b + 1, :].astype(jnp.float32), (ALIGNED_ROWS, ALIGNED_ROWS))
    query_pos = lax.broadcasted_iota(jnp.int32, key_seg.shape, 0)
    key_pos = lax.broadcasted_iota(jnp.int32, key_seg.shape, 1)
    return (query_pos >= key_pos) & (key_seg == key_seg.T)


def call(kernel, out_shape, scratch=(), cost=(10**8, 10**6), name=None, **specs):
    flops, moved = COSTS.get(name, cost)
    return pl.pallas_call(
        kernel,
        out_shape=out_shape,
        scratch_shapes=list(scratch),
        compiler_params=pltpu.CompilerParams(vmem_limit_bytes=VMEM),
        cost_estimate=pl.CostEstimate(flops=flops, bytes_accessed=moved, transcendentals=0),
        name=name,
        **specs,
    )


def bf16(*shape):
    return jax.ShapeDtypeStruct(shape, jnp.bfloat16)


LIVE, PLAN = 0, 1


def column_blocks(ref):
    return [slice(i, i + HD) for i in range(0, ref.shape[-1], HD)]


def attend(x_ref, seg_ref, out_ref, prob_ref=None):
    for b in range(2):
        rows = slice(b * ALIGNED_ROWS, (b + 1) * ALIGNED_ROWS)
        allowed = allowed_pairs(seg_ref, b)
        for h in range(HQ):
            p = block_probs(x_ref, rows, allowed, h)
            if prob_ref is not None:
                prob_ref[h, rows, :] = p
            v = x_ref[rows, QW + HD :]
            out_ref[rows, h * HD : (h + 1) * HD] = dot(p.astype(jnp.bfloat16), v, NN).astype(jnp.bfloat16)


def move(level, live, table_ref, slots_ref, block_ref, arrived_ref=None, slots_out=None):
    square = (ALIGNED_ROWS, HD)
    slot_rows = slice(0, ALIGNED_ROWS), slice(ALIGNED_ROWS, 2 * ALIGNED_ROWS)
    if arrived_ref is not None:
        top = live - table_ref[PLAN + level - 1 : PLAN + level, :]
        present = (arrived_ref[0:1, 0:HD].astype(jnp.float32) < ABSENT / 2).astype(jnp.int32)
        live = top + present
        place = jnp.where(present == 1, top, -1)
    if block_ref is not None:
        count = table_ref[PLAN + level : PLAN + level + 1, :]
        leaving = jnp.broadcast_to(jnp.where(count > 0, jnp.maximum(live - count, 0), -1), square)
    for columns in column_blocks(slots_ref):
        slots = [slots_ref[rows, columns] for rows in slot_rows]
        if arrived_ref is not None:
            arrived = arrived_ref[:, columns]
            for s in range(SLOT_NUMBER):
                slots[s] = jnp.where(jnp.broadcast_to(place, square) == s, arrived, slots[s])
                slots_out[slot_rows[s], columns] = slots[s]
        if block_ref is not None:
            block = jnp.where(leaving == 0, slots[0], jnp.full(square, ABSENT, jnp.bfloat16))
            block_ref[:, columns] = jnp.where(leaving == 1, slots[1], block)
    return live


def next_kernel(table_ref, x_ref, seg_ref, out_ref, block_ref):
    attend(x_ref, seg_ref, out_ref)
    move(0, table_ref[LIVE : LIVE + 1, :], table_ref, out_ref, block_ref)


def next_attention(table, qkv, segments):
    rows = qkv.shape[0]
    return call(next_kernel, (bf16(rows, QW), bf16(ALIGNED_ROWS, QW)), name="next_attention")(table, qkv, segments)


def move_kernel(level, table_ref, live_ref, slots_ref, arrived_ref, slots_out, live_out, block_ref):
    live_out[...] = move(level, live_ref[...], table_ref, slots_ref, block_ref, arrived_ref, slots_out)


def move_step(level, table, live, slots, block):
    arrived = swap(block, 1 << (level - 1))
    return call(
        functools.partial(move_kernel, level),
        (bf16(*slots.shape), jax.ShapeDtypeStruct((1, HD), jnp.int32), bf16(*block.shape)),
        name=f"move_step_{level}",
    )(table, live, slots, arrived)


def current_kernel(x_ref, seg_ref, order_ref, keep_ref, send_ref, prob_ref, attn_ref):
    attend(x_ref, seg_ref, attn_ref, prob_ref)
    ordered = dot(attn_ref[...], order_ref[...], NN).astype(jnp.bfloat16)
    keep_ref[...] = ordered[:, : QW // 2]
    send_ref[...] = ordered[:, QW // 2 :]


def current_attention(qkv, segments, order):
    rows = qkv.shape[0]
    return call(
        current_kernel,
        (bf16(rows, QW // 2), bf16(rows, QW // 2), jax.ShapeDtypeStruct((HQ, rows, HD), jnp.float32)),
        [pltpu.VMEM((rows, QW), jnp.bfloat16)],
        name="current_attention",
    )(qkv, segments, order)


def grad_attention_kernel(g_ref, w_ref, out_ref):
    out_ref[...] = dot(g_ref[...], w_ref[...], NT).astype(jnp.bfloat16)


def grad_attention(grad_output, weights):
    rows = grad_output.shape[0]
    return call(
        grad_attention_kernel,
        bf16(rows, QW),
        name="grad_attention",
        cost=(10**9, 5 * 10**6),
        grid=(HQ,),
        in_specs=[pl.BlockSpec((rows, D), lambda i: (0, 0)), pl.BlockSpec((HD, D), lambda i: (i, 0))],
        out_specs=pl.BlockSpec((rows, HD), lambda i: (0, i)),
    )(grad_output, weights)


def backward_kernel(x_ref, prob_ref, ga_ref, out_ref):
    for b in range(2):
        rows = slice(b * ALIGNED_ROWS, (b + 1) * ALIGNED_ROWS)
        k = x_ref[rows, QW : QW + HD]
        v = x_ref[rows, QW + HD :]
        dk = jnp.zeros((ALIGNED_ROWS, HD), jnp.float32)
        dv = jnp.zeros((ALIGNED_ROWS, HD), jnp.float32)
        for h in range(HQ):
            head = slice(h * HD, (h + 1) * HD)
            ga = ga_ref[rows, head]
            q = x_ref[rows, head]
            p = prob_ref[h, rows, :]
            dp = dot(ga, v, NT)
            ds = p * (dp - jnp.sum(p * dp, axis=-1, keepdims=True))
            high = ds.astype(jnp.bfloat16)
            low = (ds - high.astype(jnp.float32)).astype(jnp.bfloat16)
            out_ref[rows, head] = ((dot(high, k, NN) + dot(low, k, NN)) * SCALE).astype(jnp.bfloat16)
            dk += dot(high, q, TN) + dot(low, q, TN)
            dv += dot(p.astype(jnp.bfloat16), ga, TN)
        out_ref[rows, QW : QW + HD] = (dk * SCALE).astype(jnp.bfloat16)
        out_ref[rows, QW + HD :] = dv.astype(jnp.bfloat16)


def frozen_kernel(level, table_ref, live_ref, slots_ref, arrived_ref, w_ref, out_ref, moved_ref):
    @pl.when(pl.program_id(0) == 0)
    def _():
        live = move(level, live_ref[...], table_ref, slots_ref, None, arrived_ref, moved_ref)
        for columns in column_blocks(moved_ref):
            for s in range(SLOT_NUMBER):
                rows = slice(s * ALIGNED_ROWS, (s + 1) * ALIGNED_ROWS)
                block = moved_ref[rows, columns]
                dead = jnp.broadcast_to(live, block.shape) <= s
                moved_ref[rows, columns] = jnp.where(dead, jnp.zeros_like(block), block)

    out_ref[...] = dot(moved_ref[...], w_ref[...], NN).astype(jnp.bfloat16)


def frozen_projection(table, live, slots, arrived, weights):
    rows = slots.shape[0]
    width = 512

    def whole(a):
        return pl.BlockSpec(a.shape, lambda i: (0, 0))

    return call(
        functools.partial(frozen_kernel, N_DP.bit_length() - 1),
        bf16(rows, D),
        [pltpu.VMEM((rows, QW), jnp.bfloat16)],
        (10**9, 5 * 10**6),
        "frozen_projection",
        grid=(D // width,),
        in_specs=[whole(a) for a in (table, live, slots, arrived)]
        + [pl.BlockSpec((QW, width), lambda i: (0, D // width + i))],
        out_specs=pl.BlockSpec((rows, width), lambda i: (0, i)),
    )(table, live, slots, arrived, weights)


def terms_kernel(a_ref, g_ref, out_ref):
    for i in range(0, D, 512):
        columns = slice(i, i + 512)
        out_ref[:, columns] = dot(a_ref[...], g_ref[:, columns], TN).astype(jnp.bfloat16)


def terms_to_send(attention, grad_output):
    return call(terms_kernel, bf16(QW // 2, D), name="terms_to_send")(attention, grad_output)


def terms_with_kernel(a_ref, g_ref, other_ref, out_ref):
    rows = QW // N_FSDP
    for i in range(0, D, 512):
        columns = slice(i, i + 512)
        total = dot(a_ref[...], g_ref[:, columns], TN) + other_ref[:, columns].astype(jnp.float32)
        for j in range(out_ref.shape[0]):
            out_ref[j, :, columns] = total[j * rows : (j + 1) * rows].astype(jnp.bfloat16)


def terms_with_other_core(attention, grad_output, other):
    return call(terms_with_kernel, bf16(N_FSDP // 2, QW // N_FSDP, D), name="terms_with_other_core")(
        attention, grad_output, other
    )


PEERS = 8
TILES = [(i, j) for i in range(0, QW // N_FSDP, 8) for j in range(0, D, HD)]
SHARE = -(-len(TILES) // PEERS)
SHARE_ROWS = -(-SHARE * 8 // 16) * 16


def group_sum_kernel(parts_ref, out_ref):
    shares = [[] for _ in range(PEERS)]
    for n, (i, j) in enumerate(TILES):
        if i == 0:
            columns = sum(parts_ref[p, :, j : j + HD].astype(jnp.float32) for p in range(parts_ref.shape[0]))
            for r in range(0, columns.shape[0], 8):
                at = TILES.index((r, j))
                shares[at // SHARE].append((at % SHARE, columns[r : r + 8]))
    for k, share in enumerate(shares):
        tiles = [tile for _, tile in sorted(share, key=lambda pair: pair[0])]
        tiles += [jnp.zeros_like(tiles[0])] * (SHARE_ROWS // 8 - len(tiles))
        out_ref[k] = jnp.concatenate(tiles, axis=0).astype(jnp.bfloat16)


def group_sum(parts):
    return call(group_sum_kernel, bf16(PEERS, SHARE_ROWS, HD), name="group_sum")(parts)


def share_sum_kernel(parts_ref, out_ref):
    out_ref[...] = sum(parts_ref[p].astype(jnp.float32) for p in range(PEERS)).astype(jnp.bfloat16)


def share_sum(parts):
    return call(share_sum_kernel, bf16(SHARE_ROWS, HD), name="share_sum")(parts)


def mean_kernel(total_ref, other_ref, out_ref):
    total = total_ref[...].astype(jnp.float32) + other_ref[...].astype(jnp.float32)
    mean = (total * (1.0 / (N_DP * N_FSDP))).astype(jnp.bfloat16)
    for p in range(PEERS):
        out_ref[p] = mean


def mean_for_all(total, other):
    return call(mean_kernel, bf16(PEERS, SHARE_ROWS, HD), name="mean_for_all")(total, other)


def join_kernel(shares_ref, out_ref):
    shares = [shares_ref[k].astype(jnp.float32) for k in range(PEERS)]
    for j in range(0, D, HD):
        tiles = []
        for i in range(0, QW // N_FSDP, 8):
            n = TILES.index((i, j))
            row = n % SHARE * 8
            tiles.append(shares[n // SHARE][row : row + 8])
        out_ref[:, j : j + HD] = jnp.concatenate(tiles, axis=0).astype(jnp.bfloat16)


def join(shares):
    return call(join_kernel, bf16(QW // N_FSDP, D), name="join")(shares)


def side_by_side_kernel(left, right, out_ref):
    out_ref[:, :D] = left[...]
    out_ref[:, D:] = right[...]


def gather_weights(policy_out, frozen_out):
    own = call(side_by_side_kernel, bf16(policy_out.shape[0], 2 * D), name="side_by_side")(policy_out, frozen_out)
    return lax.all_gather(own, "fsdp", axis=0, tiled=True)


def fsdp_pairs(flip, x_step):
    def target(j):
        j ^= flip
        return (j & 9) | (((j >> 1 & 3) + x_step) % 4 << 1)

    return [(j, target(j)) for j in range(N_FSDP)]


def all_pairs(dp_flip, fsdp_flip):
    return [
        (d * N_FSDP + j, (d ^ dp_flip) * N_FSDP + (j ^ fsdp_flip)) for d in range(N_DP) for j in range(N_FSDP)
    ]


def swap(a, dp_flip, fsdp_flip=0):
    return lax.ppermute(a, ("dp", "fsdp"), all_pairs(dp_flip, fsdp_flip))


def add(*terms):
    return sum(t.astype(jnp.float32) for t in terms).astype(jnp.bfloat16)


def after(a, *others):
    return lax.optimization_barrier((a, *others))[0]


def sum_order(me):
    rows = QW // N_FSDP
    natural = jnp.arange(QW, dtype=jnp.int32)
    j, k = natural // rows, natural % rows
    place = ((j ^ me) & 1) * (N_FSDP // 2) + (j >> 1)
    return (natural[None, :] == (place * rows + k)[:, None]).astype(jnp.bfloat16)


def body(
    policy_out,
    frozen_out,
    qkv_current,
    segment_current,
    grad_output,
    query_key_value_next,
    document_next,
    block_counts,
    move_plan,
):
    me = lax.axis_index("fsdp")
    group = lax.axis_index("dp")
    numbers = jnp.concatenate([block_counts.reshape(1), move_plan.reshape(5), jnp.zeros((2,), jnp.int32)])
    table = jnp.broadcast_to(numbers[:, None], (8, HD))
    same_core = [[j for j in range(N_FSDP) if j & 1 == core] for core in range(2)]
    near = [[y * 16 + 4 * q + z for y in range(2) for z in range(4)] for q in range(4)]

    slots, block = next_attention(table, query_key_value_next, document_next.reshape(SLOT_NUMBER, ALIGNED_ROWS))
    live = table[LIVE : LIVE + 1]
    weights = gather_weights(after(policy_out, slots), frozen_out)
    keep_half, send_half, probs = current_attention(
        after(qkv_current, slots), segment_current.reshape(2, ALIGNED_ROWS), sum_order(me)
    )
    slots, live, block = move_step(1, table, live, slots, block)
    other = lax.ppermute(terms_to_send(after(send_half, live), grad_output), "fsdp", fsdp_pairs(1, 0))
    slots, live, block = move_step(2, table, live, slots, block)
    parts = terms_with_other_core(keep_half, grad_output, other)
    parts = lax.all_to_all(after(parts, live), "fsdp", 0, 0, axis_index_groups=same_core)
    slots, live, block = move_step(3, table, live, slots, block)
    shares = group_sum(after(parts, live))
    shares = lax.all_to_all(shares, "dp", 0, 0, axis_index_groups=near)
    slots, live, block = move_step(4, table, live, slots, block)
    total = share_sum(after(shares, live))
    total = add(total, swap(total, 4))
    block = swap(block, 16)
    shares = mean_for_all(after(total, block), swap(total, 8))
    shares = lax.all_to_all(shares, "dp", 0, 0, axis_index_groups=near)
    gradient = grad_attention(grad_output, weights)
    qkv_gradient = call(backward_kernel, bf16(*qkv_current.shape), name="backward_attention", cost=(10**9, 2 * 10**6))(
        qkv_current, probs, gradient
    )
    frozen_layer_output = frozen_projection(table, live, slots, block, weights)
    weight_grad = join(after(shares, qkv_gradient, frozen_layer_output))
    return (qkv_gradient, weight_grad, frozen_layer_output)


def solution(mesh):
    return jax.shard_map(
        body,
        mesh=mesh,
        in_specs=(
            P("fsdp", None),
            P("fsdp", None),
            P(("dp", "fsdp"), None),
            P(("dp", "fsdp")),
            P(("dp", "fsdp"), None),
            P(("dp", "fsdp"), None),
            P(("dp", "fsdp")),
            P("dp", "fsdp"),
            P("dp", "fsdp", None),
        ),
        out_specs=(P(("dp", "fsdp"), None), P("fsdp", None), P(("dp", "fsdp"), None)),
        check_vma=False,
    )
```

```python
import functools
import math

import jax
import jax.numpy as jnp
from jax import lax
from jax.experimental import pallas as pl
from jax.experimental.pallas import tpu as pltpu
from jax.sharding import PartitionSpec as P

HD = 128
HQ = 5
ALIGNED_ROWS = 128
SLOT_NUMBER = 2
QW = HQ * HD
QKV = (HQ + 2) * HD
D = 2560
SCALE = 1.0 / math.sqrt(HD)
MASKED = -1e30
ABSENT = 1024.0
COSTS = {
    name: (flops * 10**9, 0)
    for name, flops in (("move_step_1", 4), ("move_step_2", 14), ("move_step_3", 20), ("move_step_4", 16), ("outputs", 20))
}
N_DP = 32
N_FSDP = 16
VMEM = 20 * 1024 * 1024
VMEM_FROM_HBM = 58 * 1024 * 1024
FROM_HBM = ("outputs", "side_by_side", "next_attention", "move_step_1", "move_step_2", "move_step_3", "move_step_4")

NN = (((1,), (0,)), ((), ()))
NT = (((1,), (1,)), ((), ()))
TN = (((0,), (0,)), ((), ()))


def dot(a, b, dims):
    return lax.dot_general(a, b, dims, preferred_element_type=jnp.float32)


def stacked_heads(x_ref, rows):
    return jnp.concatenate([x_ref[rows, h * HD : (h + 1) * HD] for h in range(HQ)], axis=0)


def block_probs(x_ref, rows, allowed):
    s = dot(stacked_heads(x_ref, rows), x_ref[rows, QW : QW + HD], NT) * SCALE
    s = jnp.where(jnp.concatenate([allowed] * HQ, axis=0), s, MASKED)
    e = jnp.exp(s - jnp.max(s, axis=-1, keepdims=True))
    return e * (1.0 / jnp.sum(e, axis=-1, keepdims=True))


def allowed_pairs(seg_ref, b):
    key_seg = jnp.broadcast_to(seg_ref[b : b + 1, :].astype(jnp.float32), (ALIGNED_ROWS, ALIGNED_ROWS))
    query_pos = lax.broadcasted_iota(jnp.int32, key_seg.shape, 0)
    key_pos = lax.broadcasted_iota(jnp.int32, key_seg.shape, 1)
    return (query_pos >= key_pos) & (key_seg == key_seg.T)


def call(kernel, out_shape, scratch=(), cost=(10**8, 10**6), name=None, **specs):
    flops, moved = COSTS.get(name, cost)
    return pl.pallas_call(
        kernel,
        out_shape=out_shape,
        scratch_shapes=list(scratch),
        compiler_params=pltpu.CompilerParams(vmem_limit_bytes=VMEM_FROM_HBM if name in FROM_HBM else VMEM),
        cost_estimate=pl.CostEstimate(flops=flops, bytes_accessed=moved, transcendentals=0),
        name=name,
        **specs,
    )


def bf16(*shape):
    return jax.ShapeDtypeStruct(shape, jnp.bfloat16)


SMEM = pl.BlockSpec(memory_space=pltpu.SMEM)
WHOLE = pl.BlockSpec(memory_space=pltpu.VMEM)
ANY = pl.BlockSpec(memory_space=pl.ANY)


def attend(x_ref, seg_ref, out_ref, prob_ref=None):
    for b in range(2):
        rows = slice(b * ALIGNED_ROWS, (b + 1) * ALIGNED_ROWS)
        p = block_probs(x_ref, rows, allowed_pairs(seg_ref, b))
        if prob_ref is not None:
            prob_ref[b] = p
        out = dot(p.astype(jnp.bfloat16), x_ref[rows, QW + HD :], NN).astype(jnp.bfloat16)
        for h in range(HQ):
            out_ref[rows, h * HD : (h + 1) * HD] = out[h * ALIGNED_ROWS : (h + 1) * ALIGNED_ROWS]


def with_arrived(live, count, slots_ref, arrived_ref, slots_out):
    top = live - count
    present = (jnp.max(arrived_ref[0:16, 0:HD].astype(jnp.float32)) < ABSENT / 2).astype(jnp.int32)
    place = jnp.where(present == 1, top, -1)
    arrived = arrived_ref[...]
    for s in range(SLOT_NUMBER):
        rows = slice(s * ALIGNED_ROWS, (s + 1) * ALIGNED_ROWS)
        slots_out[rows, :] = jnp.where(place == s, arrived, slots_ref[rows, :])
    return top + present


def leaving_block(live, count, slots_ref):
    first, second = slots_ref[:ALIGNED_ROWS, :], slots_ref[ALIGNED_ROWS:, :]
    block = jnp.where(live - count >= 1, second, first)
    return jnp.where(count > 0, block, jnp.full_like(block, ABSENT))


def next_kernel(live_ref, plan_ref, x_ref, seg_ref, out_ref, block_ref):
    attend(x_ref, seg_ref, out_ref)
    block_ref[...] = leaving_block(live_ref[0, 0], plan_ref[0, 0, 0], out_ref)


def next_attention(live, plan, qkv, segments):
    rows = qkv.shape[0]
    return call(
        next_kernel,
        (bf16(rows, QW), bf16(ALIGNED_ROWS, QW)),
        name="next_attention",
        in_specs=[SMEM, SMEM, WHOLE, WHOLE],
    )(live, plan, qkv, segments)


def move_kernel(level, live_ref, plan_ref, slots_ref, arrived_ref, slots_out, live_out, block_ref):
    live = with_arrived(live_ref[0, 0], plan_ref[0, 0, level - 1], slots_ref, arrived_ref, slots_out)
    live_out[0, 0] = live
    block_ref[...] = leaving_block(live, plan_ref[0, 0, level], slots_out)


def move_step(level, plan, live, slots, block):
    arrived = swap(block, 1 << (level - 1))
    return call(
        functools.partial(move_kernel, level),
        (bf16(*slots.shape), jax.ShapeDtypeStruct(live.shape, jnp.int32), bf16(*block.shape)),
        name=f"move_step_{level}",
        in_specs=[SMEM, SMEM, WHOLE, WHOLE],
        out_specs=(WHOLE, SMEM, WHOLE),
    )(live, plan, slots, arrived)


def current_kernel(x_ref, seg_ref, order_ref, keep_ref, send_ref, prob_ref, attn_ref):
    attend(x_ref, seg_ref, attn_ref, prob_ref)
    ordered = dot(attn_ref[...], order_ref[...], NN).astype(jnp.bfloat16)
    keep_ref[...] = ordered[:, : QW // 2]
    send_ref[...] = ordered[:, QW // 2 :]


def current_attention(qkv, segments, order):
    rows = qkv.shape[0]
    return call(
        current_kernel,
        (bf16(rows, QW // 2), bf16(rows, QW // 2), jax.ShapeDtypeStruct((2, QW, HD), jnp.float32)),
        [pltpu.VMEM((rows, QW), jnp.bfloat16)],
        name="current_attention",
    )(qkv, segments, order)


POLICY_PARTS = (0, 256), (256, 512), (512, QW)
FROZEN_PARTS = (0, D // 2), (D // 2, D)


def outputs_kernel(
    level, live_ref, plan_ref, x_hbm, prob_hbm, g_hbm, slots_hbm, arrived_hbm, w_hbm, grad_hbm, frozen_hbm,
    x_ref, prob_ref, g_ref, slots_ref, arrived_ref, w_ref, ga_ref, grad_ref, moved_ref, frozen_ref, sems, out_sems,
):
    g_copy, x_copy, prob_copy, slots_copy, arrived_copy = (
        pltpu.make_async_copy(source, target, sems.at[i])
        for i, (source, target) in enumerate(
            ((g_hbm, g_ref), (x_hbm, x_ref), (prob_hbm, prob_ref), (slots_hbm, slots_ref), (arrived_hbm, arrived_ref))
        )
    )
    policy_copies = [
        pltpu.make_async_copy(w_hbm.at[pl.ds(i, j - i), pl.ds(0, D)], w_ref.at[pl.ds(i, j - i), pl.ds(0, D)], sems.at[5 + n])
        for n, (i, j) in enumerate(POLICY_PARTS)
    ]
    frozen_copies = [
        pltpu.make_async_copy(w_hbm.at[:, pl.ds(D + i, j - i)], w_ref.at[:, pl.ds(D + i, j - i)], sems.at[8 + n])
        for n, (i, j) in enumerate(FROZEN_PARTS)
    ]
    for copy in (g_copy, *policy_copies, x_copy, prob_copy, slots_copy, arrived_copy, *frozen_copies):
        copy.start()
    g_copy.wait()
    for copy, (i, j) in zip(policy_copies, POLICY_PARTS):
        copy.wait()
        ga_ref[:, i:j] = dot(g_ref[...], w_ref[i:j, :D], NT).astype(jnp.bfloat16)
    x_copy.wait()
    prob_copy.wait()
    for b in range(2):
        rows = slice(b * ALIGNED_ROWS, (b + 1) * ALIGNED_ROWS)
        q, ga = stacked_heads(x_ref, rows), stacked_heads(ga_ref, rows)
        k, v = x_ref[rows, QW : QW + HD], x_ref[rows, QW + HD :]
        p = prob_ref[b]
        dp = dot(ga, v, NT)
        ds = p * (dp - jnp.sum(p * dp, axis=-1, keepdims=True))
        high = ds.astype(jnp.bfloat16)
        low = (ds - high.astype(jnp.float32)).astype(jnp.bfloat16)
        dq = ((dot(high, k, NN) + dot(low, k, NN)) * SCALE).astype(jnp.bfloat16)
        for h in range(HQ):
            grad_ref[rows, h * HD : (h + 1) * HD] = dq[h * ALIGNED_ROWS : (h + 1) * ALIGNED_ROWS]
        grad_ref[rows, QW : QW + HD] = ((dot(high, q, TN) + dot(low, q, TN)) * SCALE).astype(jnp.bfloat16)
        grad_ref[rows, QW + HD :] = dot(p.astype(jnp.bfloat16), ga, TN).astype(jnp.bfloat16)
    grad_copy = pltpu.make_async_copy(grad_ref, grad_hbm, out_sems.at[0])
    grad_copy.start()
    slots_copy.wait()
    arrived_copy.wait()
    live = with_arrived(live_ref[0, 0], plan_ref[0, 0, level], slots_ref, arrived_ref, moved_ref)
    for s in range(SLOT_NUMBER):
        rows = slice(s * ALIGNED_ROWS, (s + 1) * ALIGNED_ROWS)
        block = moved_ref[rows, :]
        moved_ref[rows, :] = jnp.where(live > s, block, jnp.zeros_like(block))
    out_copies = []
    for n, (copy, (i, j)) in enumerate(zip(frozen_copies, FROZEN_PARTS)):
        copy.wait()
        frozen_ref[:, i:j] = dot(moved_ref[...], w_ref[:, D + i : D + j], NN).astype(jnp.bfloat16)
        out_copies.append(
            pltpu.make_async_copy(frozen_ref.at[:, pl.ds(i, j - i)], frozen_hbm.at[:, pl.ds(i, j - i)], out_sems.at[1 + n])
        )
        out_copies[-1].start()
    for copy in (grad_copy, *out_copies):
        copy.wait()


def outputs(level, live, plan, qkv, probs, grad_output, slots, arrived, weights):
    rows = qkv.shape[0]
    inputs = (qkv, probs, grad_output, slots, arrived, weights)
    return call(
        functools.partial(outputs_kernel, level),
        (bf16(*qkv.shape), bf16(rows, D)),
        [pltpu.VMEM(a.shape, a.dtype) for a in inputs]
        + [pltpu.VMEM((rows, QW), jnp.bfloat16), pltpu.VMEM(qkv.shape, jnp.bfloat16)]
        + [pltpu.VMEM((rows, QW), jnp.bfloat16), pltpu.VMEM((rows, D), jnp.bfloat16)]
        + [pltpu.SemaphoreType.DMA((10,)), pltpu.SemaphoreType.DMA((3,))],
        (3 * 10**9, 10**7),
        "outputs",
        in_specs=[SMEM, SMEM] + [ANY] * len(inputs),
        out_specs=(ANY, ANY),
    )(live, plan, *inputs)


def terms_kernel(a_ref, g_ref, out_ref):
    for i in range(0, D, 512):
        columns = slice(i, i + 512)
        out_ref[:, columns] = dot(a_ref[...], g_ref[:, columns], TN).astype(jnp.bfloat16)


def terms_to_send(attention, grad_output):
    return call(terms_kernel, bf16(QW // 2, D), name="terms_to_send")(attention, grad_output)


def terms_with_kernel(a_ref, g_ref, other_ref, out_ref):
    rows = QW // N_FSDP
    for i in range(0, D, 512):
        columns = slice(i, i + 512)
        total = dot(a_ref[...], g_ref[:, columns], TN) + other_ref[:, columns].astype(jnp.float32)
        for j in range(out_ref.shape[0]):
            out_ref[j, :, columns] = total[j * rows : (j + 1) * rows].astype(jnp.bfloat16)


def terms_with_other_core(attention, grad_output, other):
    return call(terms_with_kernel, bf16(N_FSDP // 2, QW // N_FSDP, D), name="terms_with_other_core")(
        attention, grad_output, other
    )


PEERS = 8
TILES = [(i, j) for i in range(0, QW // N_FSDP, 8) for j in range(0, D, HD)]
SHARE = -(-len(TILES) // PEERS)
SHARE_ROWS = -(-SHARE * 8 // 16) * 16


def group_sum_kernel(parts_ref, out_ref):
    shares = [[] for _ in range(PEERS)]
    for n, (i, j) in enumerate(TILES):
        if i == 0:
            columns = sum(parts_ref[p, :, j : j + HD].astype(jnp.float32) for p in range(parts_ref.shape[0]))
            for r in range(0, columns.shape[0], 8):
                at = TILES.index((r, j))
                shares[at // SHARE].append((at % SHARE, columns[r : r + 8]))
    for k, share in enumerate(shares):
        tiles = [tile for _, tile in sorted(share, key=lambda pair: pair[0])]
        tiles += [jnp.zeros_like(tiles[0])] * (SHARE_ROWS // 8 - len(tiles))
        out_ref[k] = jnp.concatenate(tiles, axis=0).astype(jnp.bfloat16)


def group_sum(parts):
    return call(group_sum_kernel, bf16(PEERS, SHARE_ROWS, HD), name="group_sum")(parts)


def spread_sum_kernel(scale, parts_ref, out_ref):
    total = sum(parts_ref[p].astype(jnp.float32) for p in range(parts_ref.shape[0]))
    total = (total * scale).astype(jnp.bfloat16)
    for p in range(out_ref.shape[0]):
        out_ref[p] = total


def spread_sum(parts, peers, scale, name):
    return call(functools.partial(spread_sum_kernel, scale), bf16(peers, SHARE_ROWS, HD), name=name)(parts)


def join_kernel(shares_ref, out_ref):
    shares = [shares_ref[k].astype(jnp.float32) for k in range(PEERS)]
    for j in range(0, D, HD):
        tiles = []
        for i in range(0, QW // N_FSDP, 8):
            n = TILES.index((i, j))
            row = n % SHARE * 8
            tiles.append(shares[n // SHARE][row : row + 8])
        out_ref[:, j : j + HD] = jnp.concatenate(tiles, axis=0).astype(jnp.bfloat16)


def join(shares):
    return call(join_kernel, bf16(QW // N_FSDP, D), name="join")(shares)


def side_by_side_kernel(left, right, out_ref):
    out_ref[:, :D] = left[...]
    out_ref[:, D:] = right[...]


def side_by_side(left, right):
    return call(side_by_side_kernel, bf16(left.shape[0], 2 * D), name="side_by_side")(left, right)


def fsdp_pairs(flip, x_step):
    def target(j):
        j ^= flip
        return (j & 9) | (((j >> 1 & 3) + x_step) % 4 << 1)

    return [(j, target(j)) for j in range(N_FSDP)]


def all_pairs(dp_flip, fsdp_flip):
    return [
        (d * N_FSDP + j, (d ^ dp_flip) * N_FSDP + (j ^ fsdp_flip)) for d in range(N_DP) for j in range(N_FSDP)
    ]


def swap(a, dp_flip, fsdp_flip=0):
    return lax.ppermute(a, ("dp", "fsdp"), all_pairs(dp_flip, fsdp_flip))


def add(*terms):
    return sum(t.astype(jnp.float32) for t in terms).astype(jnp.bfloat16)


def after(a, *others):
    return lax.optimization_barrier((a, *others))[0]


def sum_order(me):
    rows = QW // N_FSDP
    natural = jnp.arange(QW, dtype=jnp.int32)
    j, k = natural // rows, natural % rows
    place = ((j ^ me) & 1) * (N_FSDP // 2) + (j >> 1)
    return (natural[None, :] == (place * rows + k)[:, None]).astype(jnp.bfloat16)


def body(
    policy_out,
    frozen_out,
    qkv_current,
    segment_current,
    grad_output,
    query_key_value_next,
    document_next,
    block_counts,
    move_plan,
):
    me = lax.axis_index("fsdp")
    group = lax.axis_index("dp")
    same_core = [[j for j in range(N_FSDP) if j & 1 == core] for core in range(2)]
    near = [[y * 16 + 4 * q + z for y in range(2) for z in range(4)] for q in range(4)]
    far = [[y * 16 + 4 * q + z for q in range(4)] for y in range(2) for z in range(4)]

    own = side_by_side(policy_out, frozen_out)
    weights = lax.all_gather(own, "fsdp", axis=0, tiled=True)
    live, plan = block_counts, move_plan
    slots, block = next_attention(
        live, plan, after(query_key_value_next, own), document_next.reshape(SLOT_NUMBER, ALIGNED_ROWS)
    )
    keep_half, send_half, probs = current_attention(
        after(qkv_current, slots), segment_current.reshape(2, ALIGNED_ROWS), sum_order(me)
    )
    slots, live, block = move_step(1, plan, live, slots, block)
    other = lax.ppermute(terms_to_send(after(send_half, live), grad_output), "fsdp", fsdp_pairs(1, 0))
    parts = terms_with_other_core(keep_half, grad_output, other)
    parts = lax.all_to_all(parts, "fsdp", 0, 0, axis_index_groups=same_core)
    slots, live, block = move_step(2, plan, live, slots, block)
    shares = group_sum(after(parts, live))
    shares = lax.all_to_all(shares, "dp", 0, 0, axis_index_groups=near)
    slots, live, block = move_step(3, plan, live, slots, block)
    shares = spread_sum(after(shares, live), len(far[0]), 1.0, "near_sum")
    shares = lax.all_to_all(shares, "dp", 0, 0, axis_index_groups=far)
    shares = spread_sum(shares, PEERS, 1.0 / (N_DP * N_FSDP), "mean")
    shares = lax.all_to_all(shares, "dp", 0, 0, axis_index_groups=near)
    slots, live, block = move_step(4, plan, live, slots, block)
    block = swap(block, 16)
    qkv_gradient, frozen_layer_output = outputs(
        4, live, plan, qkv_current, probs, grad_output, slots, block, weights
    )
    weight_grad = join(after(shares, qkv_gradient))
    return (qkv_gradient, weight_grad, frozen_layer_output)


def solution(mesh):
    return jax.shard_map(
        body,
        mesh=mesh,
        in_specs=(
            P("fsdp", None),
            P("fsdp", None),
            P(("dp", "fsdp"), None),
            P(("dp", "fsdp")),
            P(("dp", "fsdp"), None),
            P(("dp", "fsdp"), None),
            P(("dp", "fsdp")),
            P("dp", "fsdp"),
            P("dp", "fsdp", None),
        ),
        out_specs=(P(("dp", "fsdp"), None), P("fsdp", None), P(("dp", "fsdp"), None)),
        check_vma=False,
    )
```

```python
import functools
import math

import jax
import jax.numpy as jnp
from jax import lax
from jax.experimental import pallas as pl
from jax.experimental.pallas import tpu as pltpu
from jax.sharding import PartitionSpec as P

HD = 128
HQ = 5
ALIGNED_ROWS = 128
SLOT_NUMBER = 2
QW = HQ * HD
QKV = (HQ + 2) * HD
D = 2560
SCALE = 1.0 / math.sqrt(HD)
MASKED = -1e30
ABSENT = 1024.0
COSTS = {
    name: (flops * 10**9, 0)
    for name, flops in (("move_step_1", 16), ("move_step_2", 10), ("move_step_3", 10), ("move_step_4", 10), ("outputs", 8))
}
N_DP = 32
N_FSDP = 16
VMEM = 20 * 1024 * 1024
VMEM_FROM_HBM = 58 * 1024 * 1024
FROM_HBM = ("outputs", "side_by_side", "next_attention")

NN = (((1,), (0,)), ((), ()))
NT = (((1,), (1,)), ((), ()))
TN = (((0,), (0,)), ((), ()))


def dot(a, b, dims):
    return lax.dot_general(a, b, dims, preferred_element_type=jnp.float32)


def stacked_heads(x_ref, rows):
    return jnp.concatenate([x_ref[rows, h * HD : (h + 1) * HD] for h in range(HQ)], axis=0)


def block_probs(x_ref, rows, allowed):
    s = dot(stacked_heads(x_ref, rows), x_ref[rows, QW : QW + HD], NT) * SCALE
    s = jnp.where(jnp.concatenate([allowed] * HQ, axis=0), s, MASKED)
    e = jnp.exp(s - jnp.max(s, axis=-1, keepdims=True))
    return e * (1.0 / jnp.sum(e, axis=-1, keepdims=True))


def allowed_pairs(seg_ref, b):
    key_seg = jnp.broadcast_to(seg_ref[b : b + 1, :].astype(jnp.float32), (ALIGNED_ROWS, ALIGNED_ROWS))
    query_pos = lax.broadcasted_iota(jnp.int32, key_seg.shape, 0)
    key_pos = lax.broadcasted_iota(jnp.int32, key_seg.shape, 1)
    return (query_pos >= key_pos) & (key_seg == key_seg.T)


def call(kernel, out_shape, scratch=(), cost=(10**8, 10**6), name=None, **specs):
    flops, moved = COSTS.get(name, cost)
    return pl.pallas_call(
        kernel,
        out_shape=out_shape,
        scratch_shapes=list(scratch),
        compiler_params=pltpu.CompilerParams(vmem_limit_bytes=VMEM_FROM_HBM if name in FROM_HBM else VMEM),
        cost_estimate=pl.CostEstimate(flops=flops, bytes_accessed=moved, transcendentals=0),
        name=name,
        **specs,
    )


def bf16(*shape):
    return jax.ShapeDtypeStruct(shape, jnp.bfloat16)


SMEM = pl.BlockSpec(memory_space=pltpu.SMEM)
WHOLE = pl.BlockSpec(memory_space=pltpu.VMEM)
ANY = pl.BlockSpec(memory_space=pl.ANY)


def column_blocks(ref):
    return [slice(i, i + HD) for i in range(0, ref.shape[-1], HD)]


def attend(x_ref, seg_ref, out_ref, prob_ref=None):
    for b in range(2):
        rows = slice(b * ALIGNED_ROWS, (b + 1) * ALIGNED_ROWS)
        p = block_probs(x_ref, rows, allowed_pairs(seg_ref, b))
        if prob_ref is not None:
            prob_ref[b] = p
        out = dot(p.astype(jnp.bfloat16), x_ref[rows, QW + HD :], NN).astype(jnp.bfloat16)
        for h in range(HQ):
            out_ref[rows, h * HD : (h + 1) * HD] = out[h * ALIGNED_ROWS : (h + 1) * ALIGNED_ROWS]


def move(level, live, table_ref, slots_ref, block_ref, arrived_ref=None, slots_out=None):
    square = (ALIGNED_ROWS, HD)
    slot_rows = slice(0, ALIGNED_ROWS), slice(ALIGNED_ROWS, 2 * ALIGNED_ROWS)
    if arrived_ref is not None:
        top = live - table_ref[level : level + 1, :]
        present = (arrived_ref[0:1, 0:HD].astype(jnp.float32) < ABSENT / 2).astype(jnp.int32)
        live = top + present
        place = jnp.where(present == 1, top, -1)
    if block_ref is not None:
        count = table_ref[level + 1 : level + 2, :]
        leaving = jnp.broadcast_to(jnp.where(count > 0, jnp.maximum(live - count, 0), -1), square)
    for columns in column_blocks(slots_ref):
        slots = [slots_ref[rows, columns] for rows in slot_rows]
        if arrived_ref is not None:
            arrived = arrived_ref[:, columns]
            for s in range(SLOT_NUMBER):
                slots[s] = jnp.where(jnp.broadcast_to(place, square) == s, arrived, slots[s])
                slots_out[slot_rows[s], columns] = slots[s]
        if block_ref is not None:
            block = jnp.where(leaving == 0, slots[0], jnp.full(square, ABSENT, jnp.bfloat16))
            block_ref[:, columns] = jnp.where(leaving == 1, slots[1], block)
    return live


def next_kernel(live_ref, plan_ref, x_ref, seg_ref, out_ref, block_ref, table_ref):
    attend(x_ref, seg_ref, out_ref)
    numbers = [live_ref[0, 0]] + [plan_ref[0, 0, level] for level in range(5)]
    for row, number in enumerate(numbers):
        table_ref[row : row + 1, :] = jnp.full((1, HD), number, jnp.int32)
    table_ref[6:8, :] = jnp.zeros((2, HD), jnp.int32)
    move(0, table_ref[0:1, :], table_ref, out_ref, block_ref)


def next_attention(live, plan, qkv, segments):
    rows = qkv.shape[0]
    return call(
        next_kernel,
        (bf16(rows, QW), bf16(ALIGNED_ROWS, QW), jax.ShapeDtypeStruct((8, HD), jnp.int32)),
        name="next_attention",
        in_specs=[SMEM, SMEM, WHOLE, WHOLE],
    )(live, plan, qkv, segments)


def move_kernel(level, table_ref, live_ref, slots_ref, arrived_ref, slots_out, live_out, block_ref):
    live_out[...] = move(level, live_ref[0:1, :], table_ref, slots_ref, block_ref, arrived_ref, slots_out)


def move_step(level, table, live, slots, block):
    arrived = swap(block, 1 << (level - 1))
    return call(
        functools.partial(move_kernel, level),
        (bf16(*slots.shape), jax.ShapeDtypeStruct((1, HD), jnp.int32), bf16(*block.shape)),
        name=f"move_step_{level}",
    )(table, live, slots, arrived)


def current_kernel(x_ref, seg_ref, order_ref, keep_ref, send_ref, prob_ref, attn_ref):
    attend(x_ref, seg_ref, attn_ref, prob_ref)
    ordered = dot(attn_ref[...], order_ref[...], NN).astype(jnp.bfloat16)
    keep_ref[...] = ordered[:, : QW // 2]
    send_ref[...] = ordered[:, QW // 2 :]


def current_attention(qkv, segments, order):
    rows = qkv.shape[0]
    return call(
        current_kernel,
        (bf16(rows, QW // 2), bf16(rows, QW // 2), jax.ShapeDtypeStruct((2, QW, HD), jnp.float32)),
        [pltpu.VMEM((rows, QW), jnp.bfloat16)],
        name="current_attention",
    )(qkv, segments, order)


POLICY_PARTS = (0, 256), (256, 512), (512, QW)
FROZEN_PARTS = (0, D // 2), (D // 2, D)


def outputs_kernel(
    level, table_ref, live_ref, x_hbm, prob_hbm, g_hbm, slots_hbm, arrived_hbm, w_hbm, grad_hbm, frozen_hbm,
    x_ref, prob_ref, g_ref, slots_ref, arrived_ref, w_ref, ga_ref, grad_ref, moved_ref, frozen_ref, sems, out_sems,
):
    g_copy, x_copy, prob_copy, slots_copy, arrived_copy = (
        pltpu.make_async_copy(source, target, sems.at[i])
        for i, (source, target) in enumerate(
            ((g_hbm, g_ref), (x_hbm, x_ref), (prob_hbm, prob_ref), (slots_hbm, slots_ref), (arrived_hbm, arrived_ref))
        )
    )
    policy_copies = [
        pltpu.make_async_copy(w_hbm.at[pl.ds(i, j - i), pl.ds(0, D)], w_ref.at[pl.ds(i, j - i), pl.ds(0, D)], sems.at[5 + n])
        for n, (i, j) in enumerate(POLICY_PARTS)
    ]
    frozen_copies = [
        pltpu.make_async_copy(w_hbm.at[:, pl.ds(D + i, j - i)], w_ref.at[:, pl.ds(D + i, j - i)], sems.at[8 + n])
        for n, (i, j) in enumerate(FROZEN_PARTS)
    ]
    for copy in (g_copy, *policy_copies, x_copy, prob_copy, slots_copy, arrived_copy, *frozen_copies):
        copy.start()
    g_copy.wait()
    for copy, (i, j) in zip(policy_copies, POLICY_PARTS):
        copy.wait()
        ga_ref[:, i:j] = dot(g_ref[...], w_ref[i:j, :D], NT).astype(jnp.bfloat16)
    x_copy.wait()
    prob_copy.wait()
    for b in range(2):
        rows = slice(b * ALIGNED_ROWS, (b + 1) * ALIGNED_ROWS)
        q, ga = stacked_heads(x_ref, rows), stacked_heads(ga_ref, rows)
        k, v = x_ref[rows, QW : QW + HD], x_ref[rows, QW + HD :]
        p = prob_ref[b]
        dp = dot(ga, v, NT)
        ds = p * (dp - jnp.sum(p * dp, axis=-1, keepdims=True))
        high = ds.astype(jnp.bfloat16)
        low = (ds - high.astype(jnp.float32)).astype(jnp.bfloat16)
        dq = ((dot(high, k, NN) + dot(low, k, NN)) * SCALE).astype(jnp.bfloat16)
        for h in range(HQ):
            grad_ref[rows, h * HD : (h + 1) * HD] = dq[h * ALIGNED_ROWS : (h + 1) * ALIGNED_ROWS]
        grad_ref[rows, QW : QW + HD] = ((dot(high, q, TN) + dot(low, q, TN)) * SCALE).astype(jnp.bfloat16)
        grad_ref[rows, QW + HD :] = dot(p.astype(jnp.bfloat16), ga, TN).astype(jnp.bfloat16)
    grad_copy = pltpu.make_async_copy(grad_ref, grad_hbm, out_sems.at[0])
    grad_copy.start()
    slots_copy.wait()
    arrived_copy.wait()
    live = move(level, live_ref[0:1, :], table_ref, slots_ref, None, arrived_ref, moved_ref)
    for columns in column_blocks(moved_ref):
        for s in range(SLOT_NUMBER):
            rows = slice(s * ALIGNED_ROWS, (s + 1) * ALIGNED_ROWS)
            block = moved_ref[rows, columns]
            alive = jnp.broadcast_to(live, block.shape) > s
            moved_ref[rows, columns] = jnp.where(alive, block, jnp.zeros_like(block))
    out_copies = []
    for n, (copy, (i, j)) in enumerate(zip(frozen_copies, FROZEN_PARTS)):
        copy.wait()
        frozen_ref[:, i:j] = dot(moved_ref[...], w_ref[:, D + i : D + j], NN).astype(jnp.bfloat16)
        out_copies.append(
            pltpu.make_async_copy(frozen_ref.at[:, pl.ds(i, j - i)], frozen_hbm.at[:, pl.ds(i, j - i)], out_sems.at[1 + n])
        )
        out_copies[-1].start()
    for copy in (grad_copy, *out_copies):
        copy.wait()


def outputs(level, table, live, qkv, probs, grad_output, slots, arrived, weights):
    rows = qkv.shape[0]
    inputs = (qkv, probs, grad_output, slots, arrived, weights)
    return call(
        functools.partial(outputs_kernel, level),
        (bf16(*qkv.shape), bf16(rows, D)),
        [pltpu.VMEM(a.shape, a.dtype) for a in inputs]
        + [pltpu.VMEM((rows, QW), jnp.bfloat16), pltpu.VMEM(qkv.shape, jnp.bfloat16)]
        + [pltpu.VMEM((rows, QW), jnp.bfloat16), pltpu.VMEM((rows, D), jnp.bfloat16)]
        + [pltpu.SemaphoreType.DMA((10,)), pltpu.SemaphoreType.DMA((3,))],
        (3 * 10**9, 10**7),
        "outputs",
        in_specs=[WHOLE, WHOLE] + [ANY] * len(inputs),
        out_specs=(ANY, ANY),
    )(table, live, *inputs)


def terms_kernel(a_ref, g_ref, out_ref):
    for i in range(0, D, 512):
        columns = slice(i, i + 512)
        out_ref[:, columns] = dot(a_ref[...], g_ref[:, columns], TN).astype(jnp.bfloat16)


def terms_to_send(attention, grad_output):
    return call(terms_kernel, bf16(QW // 2, D), name="terms_to_send")(attention, grad_output)


def terms_with_kernel(a_ref, g_ref, other_ref, out_ref):
    rows = QW // N_FSDP
    for i in range(0, D, 512):
        columns = slice(i, i + 512)
        total = dot(a_ref[...], g_ref[:, columns], TN) + other_ref[:, columns].astype(jnp.float32)
        for j in range(out_ref.shape[0]):
            out_ref[j, :, columns] = total[j * rows : (j + 1) * rows].astype(jnp.bfloat16)


def terms_with_other_core(attention, grad_output, other):
    return call(terms_with_kernel, bf16(N_FSDP // 2, QW // N_FSDP, D), name="terms_with_other_core")(
        attention, grad_output, other
    )


PEERS = 8
TILES = [(i, j) for i in range(0, QW // N_FSDP, 8) for j in range(0, D, HD)]
SHARE = -(-len(TILES) // PEERS)
SHARE_ROWS = -(-SHARE * 8 // 16) * 16


def group_sum_kernel(parts_ref, out_ref):
    shares = [[] for _ in range(PEERS)]
    for n, (i, j) in enumerate(TILES):
        if i == 0:
            columns = sum(parts_ref[p, :, j : j + HD].astype(jnp.float32) for p in range(parts_ref.shape[0]))
            for r in range(0, columns.shape[0], 8):
                at = TILES.index((r, j))
                shares[at // SHARE].append((at % SHARE, columns[r : r + 8]))
    for k, share in enumerate(shares):
        tiles = [tile for _, tile in sorted(share, key=lambda pair: pair[0])]
        tiles += [jnp.zeros_like(tiles[0])] * (SHARE_ROWS // 8 - len(tiles))
        out_ref[k] = jnp.concatenate(tiles, axis=0).astype(jnp.bfloat16)


def group_sum(parts):
    return call(group_sum_kernel, bf16(PEERS, SHARE_ROWS, HD), name="group_sum")(parts)


def spread_sum_kernel(scale, parts_ref, out_ref):
    total = sum(parts_ref[p].astype(jnp.float32) for p in range(parts_ref.shape[0]))
    total = (total * scale).astype(jnp.bfloat16)
    for p in range(out_ref.shape[0]):
        out_ref[p] = total


def spread_sum(parts, peers, scale, name):
    return call(functools.partial(spread_sum_kernel, scale), bf16(peers, SHARE_ROWS, HD), name=name)(parts)


def join_kernel(shares_ref, out_ref):
    shares = [shares_ref[k].astype(jnp.float32) for k in range(PEERS)]
    for j in range(0, D, HD):
        tiles = []
        for i in range(0, QW // N_FSDP, 8):
            n = TILES.index((i, j))
            row = n % SHARE * 8
            tiles.append(shares[n // SHARE][row : row + 8])
        out_ref[:, j : j + HD] = jnp.concatenate(tiles, axis=0).astype(jnp.bfloat16)


def join(shares):
    return call(join_kernel, bf16(QW // N_FSDP, D), name="join")(shares)


def side_by_side_kernel(left, right, out_ref):
    out_ref[:, :D] = left[...]
    out_ref[:, D:] = right[...]


def side_by_side(left, right):
    return call(side_by_side_kernel, bf16(left.shape[0], 2 * D), name="side_by_side")(left, right)


def fsdp_pairs(flip, x_step):
    def target(j):
        j ^= flip
        return (j & 9) | (((j >> 1 & 3) + x_step) % 4 << 1)

    return [(j, target(j)) for j in range(N_FSDP)]


def all_pairs(dp_flip, fsdp_flip):
    return [
        (d * N_FSDP + j, (d ^ dp_flip) * N_FSDP + (j ^ fsdp_flip)) for d in range(N_DP) for j in range(N_FSDP)
    ]


def swap(a, dp_flip, fsdp_flip=0):
    return lax.ppermute(a, ("dp", "fsdp"), all_pairs(dp_flip, fsdp_flip))


def add(*terms):
    return sum(t.astype(jnp.float32) for t in terms).astype(jnp.bfloat16)


def after(a, *others):
    return lax.optimization_barrier((a, *others))[0]


def sum_order(me):
    rows = QW // N_FSDP
    natural = jnp.arange(QW, dtype=jnp.int32)
    j, k = natural // rows, natural % rows
    place = ((j ^ me) & 1) * (N_FSDP // 2) + (j >> 1)
    return (natural[None, :] == (place * rows + k)[:, None]).astype(jnp.bfloat16)


def body(
    policy_out,
    frozen_out,
    qkv_current,
    segment_current,
    grad_output,
    query_key_value_next,
    document_next,
    block_counts,
    move_plan,
):
    me = lax.axis_index("fsdp")
    group = lax.axis_index("dp")
    same_core = [[j for j in range(N_FSDP) if j & 1 == core] for core in range(2)]
    near = [[y * 16 + 4 * q + z for y in range(2) for z in range(4)] for q in range(4)]
    far = [[y * 16 + 4 * q + z for q in range(4)] for y in range(2) for z in range(4)]

    own = side_by_side(policy_out, frozen_out)
    weights = lax.all_gather(own, "fsdp", axis=0, tiled=True)
    slots, block, table = next_attention(
        block_counts, move_plan, after(query_key_value_next, own), document_next.reshape(SLOT_NUMBER, ALIGNED_ROWS)
    )
    live = table
    keep_half, send_half, probs = current_attention(
        after(qkv_current, slots), segment_current.reshape(2, ALIGNED_ROWS), sum_order(me)
    )
    slots, live, block = move_step(1, table, live, slots, block)
    other = lax.ppermute(terms_to_send(send_half, grad_output), "fsdp", fsdp_pairs(1, 0))
    parts = terms_with_other_core(keep_half, grad_output, after(other, live))
    slots, live, block = move_step(2, table, live, slots, block)
    parts = lax.all_to_all(parts, "fsdp", 0, 0, axis_index_groups=same_core)
    slots, live, block = move_step(3, table, live, slots, block)
    shares = group_sum(after(parts, live))
    shares = lax.all_to_all(shares, "dp", 0, 0, axis_index_groups=near)
    slots, live, block = move_step(4, table, live, slots, block)
    shares = spread_sum(after(shares, live), len(far[0]), 1.0, "near_sum")
    block = swap(block, 16)
    shares = lax.all_to_all(shares, "dp", 0, 0, axis_index_groups=far)
    shares = spread_sum(shares, PEERS, 1.0 / (N_DP * N_FSDP), "mean")
    shares = lax.all_to_all(shares, "dp", 0, 0, axis_index_groups=near)
    qkv_gradient, frozen_layer_output = outputs(
        5, table, live, qkv_current, probs, grad_output, slots, block, weights
    )
    weight_grad = join(after(shares, qkv_gradient))
    return (qkv_gradient, weight_grad, frozen_layer_output)


def solution(mesh):
    return jax.shard_map(
        body,
        mesh=mesh,
        in_specs=(
            P("fsdp", None),
            P("fsdp", None),
            P(("dp", "fsdp"), None),
            P(("dp", "fsdp")),
            P(("dp", "fsdp"), None),
            P(("dp", "fsdp"), None),
            P(("dp", "fsdp")),
            P("dp", "fsdp"),
            P("dp", "fsdp", None),
        ),
        out_specs=(P(("dp", "fsdp"), None), P("fsdp", None), P(("dp", "fsdp"), None)),
        check_vma=False,
    )
```

```python
import functools
import math

import jax
import jax.numpy as jnp
from jax import lax
from jax.experimental import pallas as pl
from jax.experimental.pallas import tpu as pltpu
from jax.sharding import PartitionSpec as P

HD = 128
HQ = 5
ALIGNED_ROWS = 128
SLOT_NUMBER = 2
QW = HQ * HD
QKV = (HQ + 2) * HD
D = 2560
SCALE = 1.0 / math.sqrt(HD)
MASKED = -1e30
ABSENT = 1024.0
COSTS = {
    name: (flops * 10**9, 0)
    for name, flops in (("move_step_1", 16), ("move_step_2", 10), ("move_step_3", 10), ("move_step_4", 10), ("outputs", 8))
}
N_DP = 32
N_FSDP = 16
VMEM = 20 * 1024 * 1024
VMEM_FROM_HBM = 58 * 1024 * 1024
FROM_HBM = ("outputs", "side_by_side", "next_attention")

NN = (((1,), (0,)), ((), ()))
NT = (((1,), (1,)), ((), ()))
TN = (((0,), (0,)), ((), ()))


def dot(a, b, dims):
    return lax.dot_general(a, b, dims, preferred_element_type=jnp.float32)


def stacked_heads(x_ref, rows):
    return jnp.concatenate([x_ref[rows, h * HD : (h + 1) * HD] for h in range(HQ)], axis=0)


def block_probs(x_ref, rows, allowed):
    s = dot(stacked_heads(x_ref, rows), x_ref[rows, QW : QW + HD], NT) * SCALE
    s = jnp.where(jnp.concatenate([allowed] * HQ, axis=0), s, MASKED)
    e = jnp.exp(s - jnp.max(s, axis=-1, keepdims=True))
    return e * (1.0 / jnp.sum(e, axis=-1, keepdims=True))


def allowed_pairs(seg_ref, b):
    key_seg = jnp.broadcast_to(seg_ref[b : b + 1, :].astype(jnp.float32), (ALIGNED_ROWS, ALIGNED_ROWS))
    query_pos = lax.broadcasted_iota(jnp.int32, key_seg.shape, 0)
    key_pos = lax.broadcasted_iota(jnp.int32, key_seg.shape, 1)
    return (query_pos >= key_pos) & (key_seg == key_seg.T)


def call(kernel, out_shape, scratch=(), cost=(10**8, 10**6), name=None, **specs):
    flops, moved = COSTS.get(name, cost)
    return pl.pallas_call(
        kernel,
        out_shape=out_shape,
        scratch_shapes=list(scratch),
        compiler_params=pltpu.CompilerParams(vmem_limit_bytes=VMEM_FROM_HBM if name in FROM_HBM else VMEM),
        cost_estimate=pl.CostEstimate(flops=flops, bytes_accessed=moved, transcendentals=0),
        name=name,
        **specs,
    )


def bf16(*shape):
    return jax.ShapeDtypeStruct(shape, jnp.bfloat16)


SMEM = pl.BlockSpec(memory_space=pltpu.SMEM)
WHOLE = pl.BlockSpec(memory_space=pltpu.VMEM)
ANY = pl.BlockSpec(memory_space=pl.ANY)


def column_blocks(ref):
    return [slice(i, i + HD) for i in range(0, ref.shape[-1], HD)]


def attend(x_ref, seg_ref, out_ref, prob_ref=None):
    for b in range(2):
        rows = slice(b * ALIGNED_ROWS, (b + 1) * ALIGNED_ROWS)
        p = block_probs(x_ref, rows, allowed_pairs(seg_ref, b))
        if prob_ref is not None:
            prob_ref[b] = p
        out = dot(p.astype(jnp.bfloat16), x_ref[rows, QW + HD :], NN).astype(jnp.bfloat16)
        for h in range(HQ):
            out_ref[rows, h * HD : (h + 1) * HD] = out[h * ALIGNED_ROWS : (h + 1) * ALIGNED_ROWS]


def move(level, live, table_ref, slots_ref, block_ref, arrived_ref=None, slots_out=None):
    square = (ALIGNED_ROWS, HD)
    slot_rows = slice(0, ALIGNED_ROWS), slice(ALIGNED_ROWS, 2 * ALIGNED_ROWS)
    if arrived_ref is not None:
        top = live - table_ref[level : level + 1, :]
        present = (arrived_ref[0:1, 0:HD].astype(jnp.float32) < ABSENT / 2).astype(jnp.int32)
        live = top + present
        place = jnp.where(present == 1, top, -1)
    if block_ref is not None:
        count = table_ref[level + 1 : level + 2, :]
        leaving = jnp.broadcast_to(jnp.where(count > 0, jnp.maximum(live - count, 0), -1), square)
    for columns in column_blocks(slots_ref):
        slots = [slots_ref[rows, columns] for rows in slot_rows]
        if arrived_ref is not None:
            arrived = arrived_ref[:, columns]
            for s in range(SLOT_NUMBER):
                slots[s] = jnp.where(jnp.broadcast_to(place, square) == s, arrived, slots[s])
                slots_out[slot_rows[s], columns] = slots[s]
        if block_ref is not None:
            block = jnp.where(leaving == 0, slots[0], jnp.full(square, ABSENT, jnp.bfloat16))
            block_ref[:, columns] = jnp.where(leaving == 1, slots[1], block)
    return live


def next_kernel(live_ref, plan_ref, x_ref, seg_ref, out_ref, block_ref, table_ref):
    attend(x_ref, seg_ref, out_ref)
    numbers = [live_ref[0, 0]] + [plan_ref[0, 0, level] for level in range(5)]
    for row, number in enumerate(numbers):
        table_ref[row : row + 1, :] = jnp.full((1, HD), number, jnp.int32)
    table_ref[6:8, :] = jnp.zeros((2, HD), jnp.int32)
    move(0, table_ref[0:1, :], table_ref, out_ref, block_ref)


def next_attention(live, plan, qkv, segments):
    rows = qkv.shape[0]
    return call(
        next_kernel,
        (bf16(rows, QW), bf16(ALIGNED_ROWS, QW), jax.ShapeDtypeStruct((8, HD), jnp.int32)),
        name="next_attention",
        in_specs=[SMEM, SMEM, WHOLE, WHOLE],
    )(live, plan, qkv, segments)


def move_kernel(level, table_ref, live_ref, slots_ref, arrived_ref, slots_out, live_out, block_ref):
    live_out[...] = move(level, live_ref[0:1, :], table_ref, slots_ref, block_ref, arrived_ref, slots_out)


def move_step(level, table, live, slots, block):
    arrived = swap(block, 1 << (level - 1))
    return call(
        functools.partial(move_kernel, level),
        (bf16(*slots.shape), jax.ShapeDtypeStruct((1, HD), jnp.int32), bf16(*block.shape)),
        name=f"move_step_{level}",
    )(table, live, slots, arrived)


def current_kernel(x_ref, seg_ref, order_ref, keep_ref, send_ref, prob_ref, attn_ref):
    attend(x_ref, seg_ref, attn_ref, prob_ref)
    ordered = dot(attn_ref[...], order_ref[...], NN).astype(jnp.bfloat16)
    keep_ref[...] = ordered[:, : QW // 2]
    send_ref[...] = ordered[:, QW // 2 :]


def current_attention(qkv, segments, order):
    rows = qkv.shape[0]
    return call(
        current_kernel,
        (bf16(rows, QW // 2), bf16(rows, QW // 2), jax.ShapeDtypeStruct((2, QW, HD), jnp.float32)),
        [pltpu.VMEM((rows, QW), jnp.bfloat16)],
        name="current_attention",
    )(qkv, segments, order)


POLICY_PARTS = ((0, QW),)
FROZEN_PARTS = (0, D // 2), (D // 2, D)


def outputs_kernel(
    level, table_ref, live_ref, x_hbm, prob_hbm, g_hbm, slots_hbm, arrived_hbm, w_hbm, grad_hbm, frozen_hbm,
    x_ref, prob_ref, g_ref, slots_ref, arrived_ref, w_ref, ga_ref, grad_ref, moved_ref, frozen_ref, sems, out_sems,
):
    g_copy, x_copy, prob_copy, slots_copy, arrived_copy = (
        pltpu.make_async_copy(source, target, sems.at[i])
        for i, (source, target) in enumerate(
            ((g_hbm, g_ref), (x_hbm, x_ref), (prob_hbm, prob_ref), (slots_hbm, slots_ref), (arrived_hbm, arrived_ref))
        )
    )
    policy_copies = [
        pltpu.make_async_copy(w_hbm.at[pl.ds(i, j - i), pl.ds(0, D)], w_ref.at[pl.ds(i, j - i), pl.ds(0, D)], sems.at[5 + n])
        for n, (i, j) in enumerate(POLICY_PARTS)
    ]
    frozen_copies = [
        pltpu.make_async_copy(w_hbm.at[:, pl.ds(D + i, j - i)], w_ref.at[:, pl.ds(D + i, j - i)], sems.at[6 + n])
        for n, (i, j) in enumerate(FROZEN_PARTS)
    ]
    for copy in (g_copy, *policy_copies, x_copy, prob_copy, slots_copy, arrived_copy, *frozen_copies):
        copy.start()
    g_copy.wait()
    for copy, (i, j) in zip(policy_copies, POLICY_PARTS):
        copy.wait()
        ga_ref[:, i:j] = dot(g_ref[...], w_ref[i:j, :D], NT).astype(jnp.bfloat16)
    x_copy.wait()
    prob_copy.wait()
    for b in range(2):
        rows = slice(b * ALIGNED_ROWS, (b + 1) * ALIGNED_ROWS)
        q, ga = stacked_heads(x_ref, rows), stacked_heads(ga_ref, rows)
        k, v = x_ref[rows, QW : QW + HD], x_ref[rows, QW + HD :]
        p = prob_ref[b]
        dp = dot(ga, v, NT)
        ds = p * (dp - jnp.sum(p * dp, axis=-1, keepdims=True))
        ds = ds.astype(jnp.bfloat16)
        dq = (dot(ds, k, NN) * SCALE).astype(jnp.bfloat16)
        for h in range(HQ):
            grad_ref[rows, h * HD : (h + 1) * HD] = dq[h * ALIGNED_ROWS : (h + 1) * ALIGNED_ROWS]
        grad_ref[rows, QW : QW + HD] = (dot(ds, q, TN) * SCALE).astype(jnp.bfloat16)
        grad_ref[rows, QW + HD :] = dot(p.astype(jnp.bfloat16), ga, TN).astype(jnp.bfloat16)
    grad_copy = pltpu.make_async_copy(grad_ref, grad_hbm, out_sems.at[0])
    grad_copy.start()
    slots_copy.wait()
    arrived_copy.wait()
    live = move(level, live_ref[0:1, :], table_ref, slots_ref, None, arrived_ref, moved_ref)
    for columns in column_blocks(moved_ref):
        for s in range(SLOT_NUMBER):
            rows = slice(s * ALIGNED_ROWS, (s + 1) * ALIGNED_ROWS)
            block = moved_ref[rows, columns]
            alive = jnp.broadcast_to(live, block.shape) > s
            moved_ref[rows, columns] = jnp.where(alive, block, jnp.zeros_like(block))
    out_copies = []
    for n, (copy, (i, j)) in enumerate(zip(frozen_copies, FROZEN_PARTS)):
        copy.wait()
        frozen_ref[:, i:j] = dot(moved_ref[...], w_ref[:, D + i : D + j], NN).astype(jnp.bfloat16)
        out_copies.append(
            pltpu.make_async_copy(frozen_ref.at[:, pl.ds(i, j - i)], frozen_hbm.at[:, pl.ds(i, j - i)], out_sems.at[1 + n])
        )
        out_copies[-1].start()
    for copy in (grad_copy, *out_copies):
        copy.wait()


def outputs(level, table, live, qkv, probs, grad_output, slots, arrived, weights):
    rows = qkv.shape[0]
    inputs = (qkv, probs, grad_output, slots, arrived, weights)
    return call(
        functools.partial(outputs_kernel, level),
        (bf16(*qkv.shape), bf16(rows, D)),
        [pltpu.VMEM(a.shape, a.dtype) for a in inputs]
        + [pltpu.VMEM((rows, QW), jnp.bfloat16), pltpu.VMEM(qkv.shape, jnp.bfloat16)]
        + [pltpu.VMEM((rows, QW), jnp.bfloat16), pltpu.VMEM((rows, D), jnp.bfloat16)]
        + [pltpu.SemaphoreType.DMA((8,)), pltpu.SemaphoreType.DMA((3,))],
        (3 * 10**9, 10**7),
        "outputs",
        in_specs=[WHOLE, WHOLE] + [ANY] * len(inputs),
        out_specs=(ANY, ANY),
    )(table, live, *inputs)


def terms_kernel(a_ref, g_ref, out_ref):
    for i in range(0, D, 512):
        columns = slice(i, i + 512)
        out_ref[:, columns] = dot(a_ref[...], g_ref[:, columns], TN).astype(jnp.bfloat16)


def terms_to_send(attention, grad_output):
    return call(terms_kernel, bf16(QW // 2, D), name="terms_to_send")(attention, grad_output)


def terms_with_kernel(a_ref, g_ref, other_ref, out_ref):
    rows = QW // N_FSDP
    for i in range(0, D, 512):
        columns = slice(i, i + 512)
        total = dot(a_ref[...], g_ref[:, columns], TN) + other_ref[:, columns].astype(jnp.float32)
        for j in range(out_ref.shape[0]):
            out_ref[j, :, columns] = total[j * rows : (j + 1) * rows].astype(jnp.bfloat16)


def terms_with_other_core(attention, grad_output, other):
    return call(terms_with_kernel, bf16(N_FSDP // 2, QW // N_FSDP, D), name="terms_with_other_core")(
        attention, grad_output, other
    )


PEERS = 8
TILES = [(i, j) for i in range(0, QW // N_FSDP, 8) for j in range(0, D, HD)]
SHARE = -(-len(TILES) // PEERS)
SHARE_ROWS = -(-SHARE * 8 // 16) * 16


def group_sum_kernel(parts_ref, out_ref):
    shares = [[] for _ in range(PEERS)]
    for n, (i, j) in enumerate(TILES):
        if i == 0:
            columns = sum(parts_ref[p, :, j : j + HD].astype(jnp.float32) for p in range(parts_ref.shape[0]))
            for r in range(0, columns.shape[0], 8):
                at = TILES.index((r, j))
                shares[at // SHARE].append((at % SHARE, columns[r : r + 8]))
    for k, share in enumerate(shares):
        tiles = [tile for _, tile in sorted(share, key=lambda pair: pair[0])]
        tiles += [jnp.zeros_like(tiles[0])] * (SHARE_ROWS // 8 - len(tiles))
        out_ref[k] = jnp.concatenate(tiles, axis=0).astype(jnp.bfloat16)


def group_sum(parts):
    return call(group_sum_kernel, bf16(PEERS, SHARE_ROWS, HD), name="group_sum")(parts)


def spread_sum_kernel(scale, parts_ref, out_ref):
    total = sum(parts_ref[p].astype(jnp.float32) for p in range(parts_ref.shape[0]))
    total = (total * scale).astype(jnp.bfloat16)
    for p in range(out_ref.shape[0]):
        out_ref[p] = total


def spread_sum(parts, peers, scale, name):
    return call(functools.partial(spread_sum_kernel, scale), bf16(peers, SHARE_ROWS, HD), name=name)(parts)


def join_kernel(shares_ref, out_ref):
    shares = [shares_ref[k].astype(jnp.float32) for k in range(PEERS)]
    for j in range(0, D, HD):
        tiles = []
        for i in range(0, QW // N_FSDP, 8):
            n = TILES.index((i, j))
            row = n % SHARE * 8
            tiles.append(shares[n // SHARE][row : row + 8])
        out_ref[:, j : j + HD] = jnp.concatenate(tiles, axis=0).astype(jnp.bfloat16)


def join(shares):
    return call(join_kernel, bf16(QW // N_FSDP, D), name="join")(shares)


def side_by_side_kernel(left, right, out_ref):
    out_ref[:, :D] = left[...]
    out_ref[:, D:] = right[...]


def side_by_side(left, right):
    return call(side_by_side_kernel, bf16(left.shape[0], 2 * D), name="side_by_side")(left, right)


def fsdp_pairs(flip, x_step):
    def target(j):
        j ^= flip
        return (j & 9) | (((j >> 1 & 3) + x_step) % 4 << 1)

    return [(j, target(j)) for j in range(N_FSDP)]


def all_pairs(dp_flip, fsdp_flip):
    return [
        (d * N_FSDP + j, (d ^ dp_flip) * N_FSDP + (j ^ fsdp_flip)) for d in range(N_DP) for j in range(N_FSDP)
    ]


def swap(a, dp_flip, fsdp_flip=0):
    return lax.ppermute(a, ("dp", "fsdp"), all_pairs(dp_flip, fsdp_flip))


def add(*terms):
    return sum(t.astype(jnp.float32) for t in terms).astype(jnp.bfloat16)


def after(a, *others):
    return lax.optimization_barrier((a, *others))[0]


def sum_order(me):
    rows = QW // N_FSDP
    natural = jnp.arange(QW, dtype=jnp.int32)
    j, k = natural // rows, natural % rows
    place = ((j ^ me) & 1) * (N_FSDP // 2) + (j >> 1)
    return (natural[None, :] == (place * rows + k)[:, None]).astype(jnp.bfloat16)


def body(
    policy_out,
    frozen_out,
    qkv_current,
    segment_current,
    grad_output,
    query_key_value_next,
    document_next,
    block_counts,
    move_plan,
):
    me = lax.axis_index("fsdp")
    group = lax.axis_index("dp")
    same_core = [[j for j in range(N_FSDP) if j & 1 == core] for core in range(2)]
    near = [[y * 16 + 4 * q + z for y in range(2) for z in range(4)] for q in range(4)]
    far = [[y * 16 + 4 * q + z for q in range(4)] for y in range(2) for z in range(4)]

    own = side_by_side(policy_out, frozen_out)
    weights = lax.all_gather(own, "fsdp", axis=0, tiled=True)
    slots, block, table = next_attention(
        block_counts, move_plan, after(query_key_value_next, own), document_next.reshape(SLOT_NUMBER, ALIGNED_ROWS)
    )
    live = table
    keep_half, send_half, probs = current_attention(
        after(qkv_current, slots), segment_current.reshape(2, ALIGNED_ROWS), sum_order(me)
    )
    slots, live, block = move_step(1, table, live, slots, block)
    other = lax.ppermute(terms_to_send(send_half, grad_output), "fsdp", fsdp_pairs(1, 0))
    parts = terms_with_other_core(keep_half, grad_output, after(other, live))
    slots, live, block = move_step(2, table, live, slots, block)
    parts = lax.all_to_all(parts, "fsdp", 0, 0, axis_index_groups=same_core)
    slots, live, block = move_step(3, table, live, slots, block)
    shares = group_sum(after(parts, live))
    shares = lax.all_to_all(shares, "dp", 0, 0, axis_index_groups=near)
    slots, live, block = move_step(4, table, live, slots, block)
    shares = spread_sum(after(shares, live), len(far[0]), 1.0, "near_sum")
    block = swap(block, 16)
    shares = lax.all_to_all(shares, "dp", 0, 0, axis_index_groups=far)
    shares = spread_sum(shares, PEERS, 1.0 / (N_DP * N_FSDP), "mean")
    shares = lax.all_to_all(shares, "dp", 0, 0, axis_index_groups=near)
    qkv_gradient, frozen_layer_output = outputs(
        5, table, live, qkv_current, probs, grad_output, slots, block, weights
    )
    weight_grad = join(after(shares, qkv_gradient))
    return (qkv_gradient, weight_grad, frozen_layer_output)


def solution(mesh):
    return jax.shard_map(
        body,
        mesh=mesh,
        in_specs=(
            P("fsdp", None),
            P("fsdp", None),
            P(("dp", "fsdp"), None),
            P(("dp", "fsdp")),
            P(("dp", "fsdp"), None),
            P(("dp", "fsdp"), None),
            P(("dp", "fsdp")),
            P("dp", "fsdp"),
            P("dp", "fsdp", None),
        ),
        out_specs=(P(("dp", "fsdp"), None), P("fsdp", None), P(("dp", "fsdp"), None)),
        check_vma=False,
    )
```

```python
import functools
import math

import jax
import jax.numpy as jnp
from jax import lax
from jax.experimental import pallas as pl
from jax.experimental.pallas import tpu as pltpu
from jax.sharding import PartitionSpec as P

HD = 128
HQ = 5
ALIGNED_ROWS = 128
SLOT_NUMBER = 2
QW = HQ * HD
QKV = (HQ + 2) * HD
D = 2560
SCALE = 1.0 / math.sqrt(HD)
MASKED = -1e30
ABSENT = 1024.0
COSTS = {
    name: (flops * 10**9, 0)
    for name, flops in (("move_step_1", 16), ("move_step_2", 10), ("move_step_3", 10), ("move_step_4", 10), ("outputs", 8))
}
N_DP = 32
N_FSDP = 16
VMEM = 20 * 1024 * 1024
VMEM_FROM_HBM = 58 * 1024 * 1024
FROM_HBM = ("outputs", "side_by_side", "next_attention")

NN = (((1,), (0,)), ((), ()))
NT = (((1,), (1,)), ((), ()))
TN = (((0,), (0,)), ((), ()))


def dot(a, b, dims):
    return lax.dot_general(a, b, dims, preferred_element_type=jnp.float32)


def stacked_heads(x_ref, rows):
    return jnp.concatenate([x_ref[rows, h * HD : (h + 1) * HD] for h in range(HQ)], axis=0)


def block_probs(x_ref, rows, allowed):
    s = dot(stacked_heads(x_ref, rows), x_ref[rows, QW : QW + HD], NT) * SCALE
    s = jnp.where(jnp.concatenate([allowed] * HQ, axis=0), s, MASKED)
    e = jnp.exp(s - jnp.max(s, axis=-1, keepdims=True))
    return e * (1.0 / jnp.sum(e, axis=-1, keepdims=True))


def allowed_pairs(seg_ref, b):
    key_seg = jnp.broadcast_to(seg_ref[b : b + 1, :].astype(jnp.float32), (ALIGNED_ROWS, ALIGNED_ROWS))
    query_pos = lax.broadcasted_iota(jnp.int32, key_seg.shape, 0)
    key_pos = lax.broadcasted_iota(jnp.int32, key_seg.shape, 1)
    return (query_pos >= key_pos) & (key_seg == key_seg.T)


def call(kernel, out_shape, scratch=(), cost=(10**8, 10**6), name=None, **specs):
    flops, moved = COSTS.get(name, cost)
    return pl.pallas_call(
        kernel,
        out_shape=out_shape,
        scratch_shapes=list(scratch),
        compiler_params=pltpu.CompilerParams(vmem_limit_bytes=VMEM_FROM_HBM if name in FROM_HBM else VMEM),
        cost_estimate=pl.CostEstimate(flops=flops, bytes_accessed=moved, transcendentals=0),
        name=name,
        **specs,
    )


def bf16(*shape):
    return jax.ShapeDtypeStruct(shape, jnp.bfloat16)


SMEM = pl.BlockSpec(memory_space=pltpu.SMEM)
WHOLE = pl.BlockSpec(memory_space=pltpu.VMEM)
ANY = pl.BlockSpec(memory_space=pl.ANY)


def column_blocks(ref):
    return [slice(i, i + HD) for i in range(0, ref.shape[-1], HD)]


def attend(x_ref, seg_ref, out_ref, prob_ref=None):
    for b in range(2):
        rows = slice(b * ALIGNED_ROWS, (b + 1) * ALIGNED_ROWS)
        p = block_probs(x_ref, rows, allowed_pairs(seg_ref, b))
        if prob_ref is not None:
            prob_ref[b] = p
        out = dot(p.astype(jnp.bfloat16), x_ref[rows, QW + HD :], NN).astype(jnp.bfloat16)
        for h in range(HQ):
            out_ref[rows, h * HD : (h + 1) * HD] = out[h * ALIGNED_ROWS : (h + 1) * ALIGNED_ROWS]


def move(level, live, table_ref, slots_ref, block_ref, arrived_ref=None, slots_out=None):
    square = (ALIGNED_ROWS, HD)
    slot_rows = slice(0, ALIGNED_ROWS), slice(ALIGNED_ROWS, 2 * ALIGNED_ROWS)
    if arrived_ref is not None:
        top = live - table_ref[level : level + 1, :]
        present = (arrived_ref[0:1, 0:HD].astype(jnp.float32) < ABSENT / 2).astype(jnp.int32)
        live = top + present
        place = jnp.where(present == 1, top, -1)
    if block_ref is not None:
        count = table_ref[level + 1 : level + 2, :]
        leaving = jnp.broadcast_to(jnp.where(count > 0, jnp.maximum(live - count, 0), -1), square)
    for columns in column_blocks(slots_ref):
        slots = [slots_ref[rows, columns] for rows in slot_rows]
        if arrived_ref is not None:
            arrived = arrived_ref[:, columns]
            for s in range(SLOT_NUMBER):
                slots[s] = jnp.where(jnp.broadcast_to(place, square) == s, arrived, slots[s])
                slots_out[slot_rows[s], columns] = slots[s]
        if block_ref is not None:
            block = jnp.where(leaving == 0, slots[0], jnp.full(square, ABSENT, jnp.bfloat16))
            block_ref[:, columns] = jnp.where(leaving == 1, slots[1], block)
    return live


def next_kernel(live_ref, plan_ref, x_ref, seg_ref, out_ref, block_ref, table_ref):
    attend(x_ref, seg_ref, out_ref)
    numbers = [live_ref[0, 0]] + [plan_ref[0, 0, level] for level in range(5)]
    for row, number in enumerate(numbers):
        table_ref[row : row + 1, :] = jnp.full((1, HD), number, jnp.int32)
    table_ref[6:8, :] = jnp.zeros((2, HD), jnp.int32)
    move(0, table_ref[0:1, :], table_ref, out_ref, block_ref)


def next_attention(live, plan, qkv, segments):
    rows = qkv.shape[0]
    return call(
        next_kernel,
        (bf16(rows, QW), bf16(ALIGNED_ROWS, QW), jax.ShapeDtypeStruct((8, HD), jnp.int32)),
        name="next_attention",
        in_specs=[SMEM, SMEM, WHOLE, WHOLE],
    )(live, plan, qkv, segments)


def move_kernel(level, table_ref, live_ref, slots_ref, arrived_ref, slots_out, live_out, block_ref):
    live_out[...] = move(level, live_ref[0:1, :], table_ref, slots_ref, block_ref, arrived_ref, slots_out)


def move_step(level, table, live, slots, block):
    arrived = swap(block, 1 << (level - 1))
    return call(
        functools.partial(move_kernel, level),
        (bf16(*slots.shape), jax.ShapeDtypeStruct((1, HD), jnp.int32), bf16(*block.shape)),
        name=f"move_step_{level}",
    )(table, live, slots, arrived)


def current_kernel(x_ref, seg_ref, order_ref, keep_ref, send_ref, prob_ref, attn_ref):
    attend(x_ref, seg_ref, attn_ref, prob_ref)
    ordered = dot(attn_ref[...], order_ref[...], NN).astype(jnp.bfloat16)
    keep_ref[...] = ordered[:, : QW // 2]
    send_ref[...] = ordered[:, QW // 2 :]


def current_attention(qkv, segments, order):
    rows = qkv.shape[0]
    return call(
        current_kernel,
        (bf16(rows, QW // 2), bf16(rows, QW // 2), jax.ShapeDtypeStruct((2, QW, HD), jnp.float32)),
        [pltpu.VMEM((rows, QW), jnp.bfloat16)],
        name="current_attention",
    )(qkv, segments, order)


POLICY_PARTS = ((0, QW),)
FROZEN_PARTS = (0, D // 2), (D // 2, D)


def outputs_kernel(
    level, table_ref, live_ref, x_hbm, prob_hbm, g_hbm, slots_hbm, arrived_hbm, w_hbm, grad_hbm, frozen_hbm,
    x_ref, prob_ref, g_ref, slots_ref, arrived_ref, w_ref, ga_ref, grad_ref, moved_ref, frozen_ref, sems, out_sems,
):
    g_copy, x_copy, prob_copy, slots_copy, arrived_copy = (
        pltpu.make_async_copy(source, target, sems.at[i])
        for i, (source, target) in enumerate(
            ((g_hbm, g_ref), (x_hbm, x_ref), (prob_hbm, prob_ref), (slots_hbm, slots_ref), (arrived_hbm, arrived_ref))
        )
    )
    policy_copies = [
        pltpu.make_async_copy(w_hbm.at[pl.ds(i, j - i), pl.ds(0, D)], w_ref.at[pl.ds(i, j - i), pl.ds(0, D)], sems.at[5 + n])
        for n, (i, j) in enumerate(POLICY_PARTS)
    ]
    frozen_copies = [
        pltpu.make_async_copy(w_hbm.at[:, pl.ds(D + i, j - i)], w_ref.at[:, pl.ds(D + i, j - i)], sems.at[6 + n])
        for n, (i, j) in enumerate(FROZEN_PARTS)
    ]
    for copy in (g_copy, *policy_copies, x_copy, prob_copy, slots_copy, arrived_copy, *frozen_copies):
        copy.start()
    g_copy.wait()
    for copy, (i, j) in zip(policy_copies, POLICY_PARTS):
        copy.wait()
        ga_ref[:, i:j] = dot(g_ref[...], w_ref[i:j, :D], NT).astype(jnp.bfloat16)
    slots_copy.wait()
    arrived_copy.wait()
    live = move(level, live_ref[0:1, :], table_ref, slots_ref, None, arrived_ref, moved_ref)
    for columns in column_blocks(moved_ref):
        for s in range(SLOT_NUMBER):
            rows = slice(s * ALIGNED_ROWS, (s + 1) * ALIGNED_ROWS)
            block = moved_ref[rows, columns]
            alive = jnp.broadcast_to(live, block.shape) > s
            moved_ref[rows, columns] = jnp.where(alive, block, jnp.zeros_like(block))
    out_copies = []
    for n, (copy, (i, j)) in enumerate(zip(frozen_copies, FROZEN_PARTS)):
        copy.wait()
        frozen_ref[:, i:j] = dot(moved_ref[...], w_ref[:, D + i : D + j], NN).astype(jnp.bfloat16)
        out_copies.append(
            pltpu.make_async_copy(frozen_ref.at[:, pl.ds(i, j - i)], frozen_hbm.at[:, pl.ds(i, j - i)], out_sems.at[1 + n])
        )
        out_copies[-1].start()
    x_copy.wait()
    prob_copy.wait()
    for b in range(2):
        rows = slice(b * ALIGNED_ROWS, (b + 1) * ALIGNED_ROWS)
        q, ga = stacked_heads(x_ref, rows), stacked_heads(ga_ref, rows)
        k, v = x_ref[rows, QW : QW + HD], x_ref[rows, QW + HD :]
        p = prob_ref[b]
        dp = dot(ga, v, NT)
        ds = p * (dp - jnp.sum(p * dp, axis=-1, keepdims=True))
        ds = ds.astype(jnp.bfloat16)
        dq = (dot(ds, k, NN) * SCALE).astype(jnp.bfloat16)
        for h in range(HQ):
            grad_ref[rows, h * HD : (h + 1) * HD] = dq[h * ALIGNED_ROWS : (h + 1) * ALIGNED_ROWS]
        grad_ref[rows, QW : QW + HD] = (dot(ds, q, TN) * SCALE).astype(jnp.bfloat16)
        grad_ref[rows, QW + HD :] = dot(p.astype(jnp.bfloat16), ga, TN).astype(jnp.bfloat16)
    grad_copy = pltpu.make_async_copy(grad_ref, grad_hbm, out_sems.at[0])
    grad_copy.start()
    for copy in (grad_copy, *out_copies):
        copy.wait()


def outputs(level, table, live, qkv, probs, grad_output, slots, arrived, weights):
    rows = qkv.shape[0]
    inputs = (qkv, probs, grad_output, slots, arrived, weights)
    return call(
        functools.partial(outputs_kernel, level),
        (bf16(*qkv.shape), bf16(rows, D)),
        [pltpu.VMEM(a.shape, a.dtype) for a in inputs]
        + [pltpu.VMEM((rows, QW), jnp.bfloat16), pltpu.VMEM(qkv.shape, jnp.bfloat16)]
        + [pltpu.VMEM((rows, QW), jnp.bfloat16), pltpu.VMEM((rows, D), jnp.bfloat16)]
        + [pltpu.SemaphoreType.DMA((8,)), pltpu.SemaphoreType.DMA((3,))],
        (3 * 10**9, 10**7),
        "outputs",
        in_specs=[WHOLE, WHOLE] + [ANY] * len(inputs),
        out_specs=(ANY, ANY),
    )(table, live, *inputs)


def terms_kernel(a_ref, g_ref, out_ref):
    for i in range(0, D, 512):
        columns = slice(i, i + 512)
        out_ref[:, columns] = dot(a_ref[...], g_ref[:, columns], TN).astype(jnp.bfloat16)


def terms_to_send(attention, grad_output):
    return call(terms_kernel, bf16(QW // 2, D), name="terms_to_send")(attention, grad_output)


def terms_with_kernel(a_ref, g_ref, other_ref, out_ref):
    rows = QW // N_FSDP
    for i in range(0, D, 512):
        columns = slice(i, i + 512)
        total = dot(a_ref[...], g_ref[:, columns], TN) + other_ref[:, columns].astype(jnp.float32)
        for j in range(out_ref.shape[0]):
            out_ref[j, :, columns] = total[j * rows : (j + 1) * rows].astype(jnp.bfloat16)


def terms_with_other_core(attention, grad_output, other):
    return call(terms_with_kernel, bf16(N_FSDP // 2, QW // N_FSDP, D), name="terms_with_other_core")(
        attention, grad_output, other
    )


PEERS = 8
TILES = [(i, j) for i in range(0, QW // N_FSDP, 8) for j in range(0, D, HD)]
SHARE = -(-len(TILES) // PEERS)
SHARE_ROWS = -(-SHARE * 8 // 16) * 16


def group_sum_kernel(parts_ref, out_ref):
    shares = [[] for _ in range(PEERS)]
    for n, (i, j) in enumerate(TILES):
        if i == 0:
            columns = sum(parts_ref[p, :, j : j + HD].astype(jnp.float32) for p in range(parts_ref.shape[0]))
            for r in range(0, columns.shape[0], 8):
                at = TILES.index((r, j))
                shares[at // SHARE].append((at % SHARE, columns[r : r + 8]))
    for k, share in enumerate(shares):
        tiles = [tile for _, tile in sorted(share, key=lambda pair: pair[0])]
        tiles += [jnp.zeros_like(tiles[0])] * (SHARE_ROWS // 8 - len(tiles))
        out_ref[k] = jnp.concatenate(tiles, axis=0).astype(jnp.bfloat16)


def group_sum(parts):
    return call(group_sum_kernel, bf16(PEERS, SHARE_ROWS, HD), name="group_sum")(parts)


def spread_sum_kernel(scale, parts_ref, out_ref):
    total = sum(parts_ref[p].astype(jnp.float32) for p in range(parts_ref.shape[0]))
    total = (total * scale).astype(jnp.bfloat16)
    for p in range(out_ref.shape[0]):
        out_ref[p] = total


def spread_sum(parts, peers, scale, name):
    return call(functools.partial(spread_sum_kernel, scale), bf16(peers, SHARE_ROWS, HD), name=name)(parts)


def join_kernel(shares_ref, out_ref):
    shares = [shares_ref[k].astype(jnp.float32) for k in range(PEERS)]
    for j in range(0, D, HD):
        tiles = []
        for i in range(0, QW // N_FSDP, 8):
            n = TILES.index((i, j))
            row = n % SHARE * 8
            tiles.append(shares[n // SHARE][row : row + 8])
        out_ref[:, j : j + HD] = jnp.concatenate(tiles, axis=0).astype(jnp.bfloat16)


def join(shares):
    return call(join_kernel, bf16(QW // N_FSDP, D), name="join")(shares)


def side_by_side_kernel(left, right, out_ref):
    out_ref[:, :D] = left[...]
    out_ref[:, D:] = right[...]


def side_by_side(left, right):
    return call(side_by_side_kernel, bf16(left.shape[0], 2 * D), name="side_by_side")(left, right)


def fsdp_pairs(flip, x_step):
    def target(j):
        j ^= flip
        return (j & 9) | (((j >> 1 & 3) + x_step) % 4 << 1)

    return [(j, target(j)) for j in range(N_FSDP)]


def all_pairs(dp_flip, fsdp_flip):
    return [
        (d * N_FSDP + j, (d ^ dp_flip) * N_FSDP + (j ^ fsdp_flip)) for d in range(N_DP) for j in range(N_FSDP)
    ]


def swap(a, dp_flip, fsdp_flip=0):
    return lax.ppermute(a, ("dp", "fsdp"), all_pairs(dp_flip, fsdp_flip))


def add(*terms):
    return sum(t.astype(jnp.float32) for t in terms).astype(jnp.bfloat16)


def after(a, *others):
    return lax.optimization_barrier((a, *others))[0]


def sum_order(me):
    rows = QW // N_FSDP
    natural = jnp.arange(QW, dtype=jnp.int32)
    j, k = natural // rows, natural % rows
    place = ((j ^ me) & 1) * (N_FSDP // 2) + (j >> 1)
    return (natural[None, :] == (place * rows + k)[:, None]).astype(jnp.bfloat16)


def body(
    policy_out,
    frozen_out,
    qkv_current,
    segment_current,
    grad_output,
    query_key_value_next,
    document_next,
    block_counts,
    move_plan,
):
    me = lax.axis_index("fsdp")
    group = lax.axis_index("dp")
    same_core = [[j for j in range(N_FSDP) if j & 1 == core] for core in range(2)]
    near = [[y * 16 + 4 * q + z for y in range(2) for z in range(4)] for q in range(4)]
    far = [[y * 16 + 4 * q + z for q in range(4)] for y in range(2) for z in range(4)]

    own = side_by_side(policy_out, frozen_out)
    weights = lax.all_gather(own, "fsdp", axis=0, tiled=True)
    slots, block, table = next_attention(
        block_counts, move_plan, after(query_key_value_next, own), document_next.reshape(SLOT_NUMBER, ALIGNED_ROWS)
    )
    live = table
    keep_half, send_half, probs = current_attention(
        after(qkv_current, slots), segment_current.reshape(2, ALIGNED_ROWS), sum_order(me)
    )
    slots, live, block = move_step(1, table, live, slots, block)
    other = lax.ppermute(terms_to_send(send_half, grad_output), "fsdp", fsdp_pairs(1, 0))
    parts = terms_with_other_core(keep_half, grad_output, after(other, live))
    slots, live, block = move_step(2, table, live, slots, block)
    parts = lax.all_to_all(parts, "fsdp", 0, 0, axis_index_groups=same_core)
    slots, live, block = move_step(3, table, live, slots, block)
    shares = group_sum(after(parts, live))
    shares = lax.all_to_all(shares, "dp", 0, 0, axis_index_groups=near)
    slots, live, block = move_step(4, table, live, slots, block)
    shares = spread_sum(after(shares, live), len(far[0]), 1.0, "near_sum")
    block = swap(block, 16)
    shares = lax.all_to_all(shares, "dp", 0, 0, axis_index_groups=far)
    shares = spread_sum(shares, PEERS, 1.0 / (N_DP * N_FSDP), "mean")
    shares = lax.all_to_all(shares, "dp", 0, 0, axis_index_groups=near)
    qkv_gradient, frozen_layer_output = outputs(
        5, table, live, qkv_current, probs, grad_output, slots, block, weights
    )
    weight_grad = join(after(shares, qkv_gradient))
    return (qkv_gradient, weight_grad, frozen_layer_output)


def solution(mesh):
    return jax.shard_map(
        body,
        mesh=mesh,
        in_specs=(
            P("fsdp", None),
            P("fsdp", None),
            P(("dp", "fsdp"), None),
            P(("dp", "fsdp")),
            P(("dp", "fsdp"), None),
            P(("dp", "fsdp"), None),
            P(("dp", "fsdp")),
            P("dp", "fsdp"),
            P("dp", "fsdp", None),
        ),
        out_specs=(P(("dp", "fsdp"), None), P("fsdp", None), P(("dp", "fsdp"), None)),
        check_vma=False,
    )
```
